256 devices in a mesh: dp: 16 (over z, core), mp: 16 (over y, x).
Axes of the slice: x: 4, y: 4, z: 8, core: 2. Of those that a mesh axis runs over, the one named last changes fastest.
Arguments:
- features: bfloat16 [6144, 2048], P('dp', 'mp'), may hold values from -6 to 6
- w_in: bfloat16 [2048, 16384], P('dp', 'mp'), may hold values from -0.125 to 0.125
- w_out: bfloat16 [16384, 2048], P('mp', 'dp'), may hold values from -0.0625 to 0.0625
- unit_order: int32 [16384], P('mp'), may hold values from 0 to 16383, as said below
- cotangents: bfloat16 [4, 6144, 2048], P(None, 'dp', 'mp'), may hold values from -6 to 6
Outputs:
- outputs: bfloat16 [4, 6144, 2048], P(None, 'dp', 'mp')
- grad_features: bfloat16 [6144, 2048], P('dp', 'mp')
- grad_in: bfloat16 [2048, 16384], P('dp', 'mp')
- grad_out: bfloat16 [16384, 2048], P('mp', 'dp')
The draws below stay inside these ranges and needn't reach their ends.
Inputs may be any that keep to these rules, and one draw needn't show every extreme that they name: `unit_order`: A permutation of 0 to 16383; every block of 1024 consecutive stored positions holds exactly 128 units below 2048, 128 from 2048 to 4096, 256 from 4096 to 8192 and 512 from 8192 up.
All inputs are finite; a program needn't handle non-finite values.
Results may differ from the reference program's by a relative error of at most 0.023.
Values may be sent and summed in bfloat16 or wider, within the bound.
No kernel may reach another device: no remote copies, remote signals or barrier semaphores. Data moves between devices by JAX's collectives and lax.ppermute only.
A program may use at most 128 MiB of HBM per device.

```python
import jax
import jax.numpy as jnp
from jax import lax

D = 2048
FF = 16384
TOK_DEV = 384
TOKENS = 6144
FF_DEV = 1024
N_DP = 16
N_MP = 16


def draw_unit_order(key, part):
    key = jax.random.fold_in(key, 11)
    shards = FF // FF_DEV
    split_one, split_two = jax.random.split(key)
    residues = jax.random.permutation(split_one, shards)
    lane_ids = jnp.arange(FF_DEV, dtype=jnp.int32)
    stored = lane_ids[None, :] * shards + residues[:, None]
    scores = jax.random.randint(split_two, (shards, FF_DEV), 0, 4096) * FF_DEV + lane_ids[None, :]
    ranking = jnp.argsort(scores, axis=1)
    stored = jnp.take_along_axis(stored, ranking, axis=1)
    return stored.reshape(FF).astype(jnp.int32)


def block_scale(stream_key, dims, pieces, smallest, high):
    level, own = 1.0, jax.random.fold_in(stream_key, 6)
    for dim, shards_of in pieces:
        steps = jnp.exp(jax.random.uniform(jax.random.fold_in(own, dim), (shards_of,), jnp.float32, smallest / len(pieces), high / len(pieces)))
        level = level * jnp.repeat(steps, dims[dim] // shards_of).reshape([-1 if axis == dim else 1 for axis in range(len(dims))])
    return level


def normal_values(own_key, extent, scale, bound, pieces=(), kind=jnp.bfloat16):
    factor_of = block_scale(own_key, extent, pieces, -0.22, 0.18) if pieces else 1.0
    drawn = jax.random.normal(own_key, extent, jnp.float32) * scale * factor_of
    return jnp.minimum(jnp.maximum(drawn, -bound), bound).astype(kind)


def setup_inputs(seed: int = 0) -> dict:
    key_of = jax.random.split(jax.random.key(seed), 6)
    return {
        "features": normal_values(key_of[0], (TOKENS, D), 1.0, 6.0, ((0, 16), (1, 16))),
        "w_in": normal_values(key_of[1], (D, FF), D ** -0.5, 0.125, ((0, 16), (1, 16))),
        "w_out": normal_values(key_of[2], (FF, D), (FF // 2) ** -0.5, 0.0625, ((0, 16), (1, 16))),
        "unit_order": draw_unit_order(jax.random.fold_in(key_of[5], 71), 0),
        "cotangents": normal_values(key_of[4], (4, TOKENS, D), 1.0, 6.0, ((1, 16), (2, 16))),
    }


tanh_scale = 0.7978845608
cubic_term = 0.044715


def gelu_value(value):
    inner = tanh_scale * (value + cubic_term * value * value * value)
    return 0.5 * value * (1.0 + jnp.tanh(inner))


def gelu_slope(value):
    tangent = jnp.tanh(tanh_scale * (value + cubic_term * value * value * value))
    return 0.5 * (1.0 + tangent) + 0.5 * value * (1.0 - tangent * tangent) * tanh_scale * (1.0 + 3.0 * cubic_term * value * value)


def arrange(stored_units):
    local_width = stored_units.shape[0]
    band_ids = (stored_units >= FF // 8).astype(jnp.int32) + (stored_units >= FF // 4).astype(jnp.int32) + (stored_units >= FF // 2).astype(jnp.int32)
    ranking = jnp.argsort(band_ids * local_width + jnp.arange(local_width, dtype=jnp.int32))
    return ranking, jnp.argsort(ranking)


def band_limits(local_width):
    eighth = local_width // 8
    return [(0, eighth), (eighth, 2 * eighth), (2 * eighth, 4 * eighth), (4 * eighth, local_width)]


def round_trip(value):
    return lax.optimization_barrier(value.astype(jnp.bfloat16)).astype(jnp.float32)


def reference(features, w_in, w_out, unit_order, cotangents):
    local_width = FF // N_MP
    limits = band_limits(local_width)
    combined = jnp.cumsum(cotangents.astype(jnp.float32)[::-1], axis=0)[::-1].astype(jnp.bfloat16)
    grouped_x = features.reshape(N_DP, TOK_DEV, D).astype(jnp.float32)

    def block(running, block_index):
        out_sum, dx_sum = running
        start_at = block_index * local_width
        in_columns = lax.dynamic_slice_in_dim(w_in, start_at, local_width, 1)
        out_rows = lax.dynamic_slice_in_dim(w_out, start_at, local_width, 0)
        stored_units = lax.dynamic_slice_in_dim(unit_order, start_at, local_width, 0)
        ranking, inverse = arrange(stored_units)
        in_columns = jnp.take(in_columns, ranking, axis=1)
        out_rows = jnp.take(out_rows, ranking, axis=0)
        pre = jnp.dot(features, in_columns, preferred_element_type=jnp.float32)
        hidden = gelu_value(pre).astype(jnp.bfloat16)
        products = [jnp.dot(hidden[:, lo:hi], out_rows[lo:hi], preferred_element_type=jnp.float32) for lo, hi in limits]
        partial_out = []
        acc = jnp.zeros_like(products[0])
        for term in products:
            acc = acc + term
            partial_out.append(round_trip(acc))
        out_sum = out_sum + jnp.stack(partial_out)
        grad_hidden = jnp.concatenate([lax.dot_general(combined[level], out_rows[lo:hi], (((1,), (1,)), ((), ())), preferred_element_type=jnp.float32) for level, (lo, hi) in enumerate(limits)], axis=1)
        grad_pre = (grad_hidden * gelu_slope(pre)).astype(jnp.bfloat16)
        dx_sum = dx_sum + lax.dot_general(grad_pre, in_columns, (((1,), (1,)), ((), ())), preferred_element_type=jnp.float32)
        grouped_pre = grad_pre.reshape(N_DP, TOK_DEV, local_width).astype(jnp.float32)
        grad_in_part = jnp.einsum("gtd,gtf->gdf", grouped_x, grouped_pre, precision=lax.Precision.HIGHEST)
        grad_in_block = jnp.sum(round_trip(grad_in_part), axis=0).astype(jnp.bfloat16)
        grouped_hidden = hidden.reshape(N_DP, TOK_DEV, local_width).astype(jnp.float32)
        pieces_out = []
        for level, (lo, hi) in enumerate(limits):
            grouped_comb = combined[level].reshape(N_DP, TOK_DEV, D).astype(jnp.float32)
            term = jnp.einsum("gtf,gtd->gfd", grouped_hidden[:, :, lo:hi], grouped_comb, precision=lax.Precision.HIGHEST)
            pieces_out.append(jnp.sum(round_trip(term), axis=0))
        grad_out_block = jnp.concatenate(pieces_out, axis=0).astype(jnp.bfloat16)
        grad_in_block = jnp.take(grad_in_block, inverse, axis=1)
        grad_out_block = jnp.take(grad_out_block, inverse, axis=0)
        return (out_sum, dx_sum), (grad_in_block, grad_out_block)

    initial = (jnp.zeros((4, TOKENS, D), jnp.float32), jnp.zeros((TOKENS, D), jnp.float32))
    (out_sum, dx_sum), (grad_in_blocks, grad_out_blocks) = lax.scan(block, initial, jnp.arange(N_MP, dtype=jnp.int32))
    grad_in = jnp.transpose(grad_in_blocks, (1, 0, 2)).reshape(D, FF)
    grad_out = grad_out_blocks.reshape(FF, D)
    return out_sum.astype(jnp.bfloat16), dx_sum.astype(jnp.bfloat16), grad_in, grad_out
```

```python
import functools

import jax
import jax.numpy as jnp
from jax import lax
from jax.experimental import pallas as pl
from jax.experimental.pallas import tpu as pltpu
from jax.sharding import Mesh, PartitionSpec as P

FF = 16384
MP = 16
Z = 8
SHARE = 64
HALF = SHARE // 2
UNITS = MP * HALF
LAST_OF_BAND = (1, 3, 7, 15)

tanh_scale = 0.7978845608
cubic_term = 0.044715

F32 = jnp.float32
BF16 = jnp.bfloat16
MXN = (((1,), (1,)), ((), ()))
TN = (((0,), (0,)), ((), ()))


def params(mib=48):
    return pltpu.CompilerParams(vmem_limit_bytes=mib << 20)


def one_hot(places):
    size = places.shape[1]
    return (lax.broadcasted_iota(jnp.int32, (size, size), 0) == places).astype(BF16)


def sort_kernel(core_ref, units_ref, w_in_ref, w_out_ref, own_ref, other_ref, places_ref):
    units = units_ref[...]
    size = units.shape[1]
    band = (
        (units >= FF // 8).astype(jnp.int32)
        + (units >= FF // 4).astype(jnp.int32)
        + (units >= FF // 2).astype(jnp.int32)
    )
    rows = lax.broadcasted_iota(jnp.int32, (8, size), 0)
    member = rows == band
    before = (
        lax.broadcasted_iota(jnp.int32, (size, size), 0)
        < lax.broadcasted_iota(jnp.int32, (size, size), 1)
    ).astype(BF16)
    count = jnp.dot(member.astype(BF16), before, preferred_element_type=F32)
    base = jnp.where(rows == 0, 0, jnp.where(rows == 1, size // 8, jnp.where(rows == 2, size // 4, size // 2)))
    rank = jnp.sum(jnp.where(member, count + base.astype(F32), 0.0), axis=0, keepdims=True).astype(jnp.int32)
    dest = rank // SHARE
    within = rank % SHARE
    half = within // HALF
    places = jnp.where(half == core_ref[0], 0, UNITS) + dest * HALF + within % HALF
    places_ref[...] = places
    picks = one_hot(places)
    rows_in = lax.dot_general(picks, w_in_ref[...], MXN, preferred_element_type=F32).astype(BF16)
    rows_out = jnp.dot(picks, w_out_ref[...], preferred_element_type=F32).astype(BF16)
    for k in range(MP):
        lo = k * HALF
        own_ref[k, 0] = rows_in[lo : lo + HALF]
        own_ref[k, 1] = rows_out[lo : lo + HALF]
        other_ref[k, 0] = rows_in[UNITS + lo : UNITS + lo + HALF]
        other_ref[k, 1] = rows_out[UNITS + lo : UNITS + lo + HALF]


def unsort_kernel(places_ref, own_ref, other_ref, grad_in_ref, grad_out_ref):
    picks = one_hot(places_ref[...])

    def rows(i):
        return jnp.concatenate([own_ref[k, i] for k in range(MP)] + [other_ref[k, i] for k in range(MP)], axis=0)

    grad_in_ref[...] = lax.dot_general(rows(0), picks, TN, preferred_element_type=F32).astype(BF16)
    grad_out_ref[...] = lax.dot_general(rows(1), picks, TN, preferred_element_type=F32).T.astype(BF16)


def tokens_kernel(x_ref, cot_ref, send_ref):
    x = x_ref[...]
    total = cot_ref[3].astype(F32)
    combined = [None] * 4
    combined[3] = cot_ref[3]
    for b in (2, 1, 0):
        total = total + cot_ref[b].astype(F32)
        combined[b] = total.astype(BF16)
    first = 0
    for b, last in enumerate(LAST_OF_BAND):
        for k in range(first, last + 1):
            send_ref[k, 0] = x
            send_ref[k, 1] = combined[b]
        first = last + 1


def grads_kernel(
    own_ref, peer_ref, weights_ref, grads_ref, hidden_ref, grad_pre_ref,
    x_ref, comb_ref, in_ref, out_ref, part_ref, hid_ref, gpre_ref, token_sem, weight_sem, grad_sem, keep_sem,
):
    count = own_ref.shape[1]
    loads = []
    for half, ref in enumerate((own_ref, peer_ref)):
        for i, to in enumerate((x_ref, comb_ref)):
            loads.append(
                pltpu.make_async_copy(ref.at[i], to.at[pl.ds(half * count, count)], token_sem.at[2 * half + i])
            )
    width = weights_ref.shape[-1]
    for z in range(Z):
        for i, to in enumerate((in_ref, out_ref)):
            loads.append(
                pltpu.make_async_copy(
                    weights_ref.at[z, :, i], to.at[:, :, pl.ds(z * width, width)], weight_sem.at[2 * z + i]
                )
            )
    for load in loads:
        load.start()
    for load in loads:
        load.wait()
    full = in_ref.shape[-1]
    w_in = in_ref[...].reshape(UNITS, full)
    w_out = out_ref[...].reshape(UNITS, full)
    step = 256
    for lo in range(0, 2 * count, step):
        pre = lax.dot_general(w_in, x_ref[lo : lo + step], MXN, preferred_element_type=F32)
        back = lax.dot_general(w_out, comb_ref[lo : lo + step], MXN, preferred_element_type=F32)
        square = pre * pre
        tangent = jnp.tanh(tanh_scale * (pre + cubic_term * square * pre))
        hid_ref[:, lo : lo + step] = (0.5 * pre * (1.0 + tangent)).astype(BF16)
        slope = 0.5 * (1.0 + tangent) + 0.5 * pre * (1.0 - tangent * tangent) * tanh_scale * (
            1.0 + 3.0 * cubic_term * square
        )
        gpre_ref[:, lo : lo + step] = (back * slope).astype(BF16)
    keeps = [
        pltpu.make_async_copy(hid_ref, hidden_ref, keep_sem.at[0]),
        pltpu.make_async_copy(gpre_ref, grad_pre_ref, keep_sem.at[1]),
    ]
    for keep in keeps:
        keep.start()
    stores = []
    for z in range(Z):
        lo = z * width
        grad_in = jnp.dot(gpre_ref[...], x_ref[:, lo : lo + width], preferred_element_type=F32)
        grad_out = jnp.dot(hid_ref[...], comb_ref[:, lo : lo + width], preferred_element_type=F32)
        part_ref[z, :, 0] = grad_in.astype(BF16).reshape(MP, HALF, width)
        part_ref[z, :, 1] = grad_out.astype(BF16).reshape(MP, HALF, width)
        store = pltpu.make_async_copy(part_ref.at[z], grads_ref.at[z], grad_sem.at[z])
        store.start()
        stores.append(store)
    for copy in keeps + stores:
        copy.wait()


def project_kernel(hidden_ref, grad_pre_ref, weights_ref, own_ref, other_ref, hid_ref, gpre_ref):
    @pl.when(pl.program_id(0) == 0)
    def _():
        hid_ref[...] = hidden_ref[...].T
        gpre_ref[...] = grad_pre_ref[...].T

    width = weights_ref.shape[-1]
    w_in = weights_ref[0, :, 0].reshape(UNITS, width)
    w_out = weights_ref[0, :, 1].reshape(UNITS, width)
    for i, (left, right) in enumerate(((hid_ref, w_out), (gpre_ref, w_in))):
        whole = jnp.dot(left[...], right, preferred_element_type=F32).astype(BF16)
        count = whole.shape[0] // 2
        part = width // 2
        for side in range(2):
            own_ref[side, i] = whole[:count, side * part : (side + 1) * part]
            other_ref[side, i] = whole[count:, side * part : (side + 1) * part]


def sums_kernel(got_ref, outputs_ref, dx_ref):
    total = jnp.zeros(dx_ref.shape, F32)
    for k in range(MP):
        total = total + got_ref[k, 0].astype(F32)
        if k in LAST_OF_BAND:
            outputs_ref[LAST_OF_BAND.index(k)] = total.astype(BF16)
    total = jnp.zeros(dx_ref.shape, F32)
    for k in range(MP):
        total = total + got_ref[k, 1].astype(F32)
    dx_ref[...] = total.astype(BF16)


ANY = pl.BlockSpec(memory_space=pl.ANY)
VMEM = pl.BlockSpec(memory_space=pltpu.VMEM)
SMEM = pl.BlockSpec(memory_space=pltpu.SMEM)


def struct(*shape, dtype=BF16):
    return jax.ShapeDtypeStruct(shape, dtype)


def to_other_core(value):
    return lax.ppermute(value, "core", [(0, 1), (1, 0)])


def exchange(value):
    return lax.all_to_all(value, ("y", "x"), 0, 0, tiled=True)


def after(value, earlier):
    return lax.optimization_barrier((value, earlier))[0]


def per_device(features, w_in, w_out, unit_order, cotangents):
    core = lax.axis_index("core")
    count, part = features.shape
    units = unit_order.shape[0]
    width = 2 * part
    full = MP * part
    own, other, places = pl.pallas_call(
        sort_kernel,
        out_shape=(
            struct(MP, 2, HALF, part),
            struct(MP, 2, HALF, part),
            struct(1, units, dtype=jnp.int32),
        ),
        in_specs=[SMEM, VMEM, VMEM, VMEM],
        out_specs=(VMEM, VMEM, VMEM),
        compiler_params=params(),
        name="sort_units",
    )(core.reshape(1), unit_order.reshape(1, units), w_in, w_out)
    got = to_other_core(other)
    both = jnp.where(core == 0, jnp.concatenate([own, got], axis=3), jnp.concatenate([got, own], axis=3))
    mine = exchange(both)
    weights = lax.all_gather(mine.reshape(2 * UNITS, width), "z", axis=0, tiled=True)
    weights = weights.reshape(Z, MP, 2, HALF, width)

    send = pl.pallas_call(
        tokens_kernel,
        out_shape=struct(MP, 2, count, part),
        in_specs=[VMEM, VMEM],
        out_specs=VMEM,
        compiler_params=params(),
        name="combine_cotangents",
    )(features, cotangents)
    tokens = exchange(after(send, mine))
    tokens = tokens.transpose(1, 2, 0, 3).reshape(2, count, full)
    peer_tokens = to_other_core(tokens)

    grads, hidden, grad_pre = pl.pallas_call(
        grads_kernel,
        out_shape=(
            struct(Z, MP, 2, HALF, width),
            struct(UNITS, 2 * count),
            struct(UNITS, 2 * count),
        ),
        in_specs=[ANY] * 3,
        out_specs=(ANY,) * 3,
        scratch_shapes=[
            pltpu.VMEM((2 * count, full), BF16),
            pltpu.VMEM((2 * count, full), BF16),
            pltpu.VMEM((MP, HALF, full), BF16),
            pltpu.VMEM((MP, HALF, full), BF16),
            pltpu.VMEM((Z, MP, 2, HALF, width), BF16),
            pltpu.VMEM((UNITS, 2 * count), BF16),
            pltpu.VMEM((UNITS, 2 * count), BF16),
            pltpu.SemaphoreType.DMA((4,)),
            pltpu.SemaphoreType.DMA((2 * Z,)),
            pltpu.SemaphoreType.DMA((Z,)),
            pltpu.SemaphoreType.DMA((2,)),
        ],
        compiler_params=params(),
        cost_estimate=pl.CostEstimate(flops=8 * UNITS * 2 * count * full, bytes_accessed=16 << 20, transcendentals=UNITS * 2 * count),
        name="hidden_and_weight_grads",
    )(tokens, peer_tokens, weights)
    summed = lax.psum_scatter(grads.reshape(Z * 2 * UNITS, width), "z", scatter_dimension=0, tiled=True)
    summed = summed.reshape(MP, 2, HALF, width)

    out_own, out_other = pl.pallas_call(
        project_kernel,
        grid=(Z,),
        out_shape=(struct(MP, 2, count, part), struct(MP, 2, count, part)),
        in_specs=[
            pl.BlockSpec((UNITS, 2 * count), lambda z: (0, 0)),
            pl.BlockSpec((UNITS, 2 * count), lambda z: (0, 0)),
            pl.BlockSpec((1, MP, 2, HALF, width), lambda z: (z, 0, 0, 0, 0)),
        ],
        out_specs=(
            pl.BlockSpec((2, 2, count, part), lambda z: (z, 0, 0, 0)),
            pl.BlockSpec((2, 2, count, part), lambda z: (z, 0, 0, 0)),
        ),
        scratch_shapes=[pltpu.VMEM((2 * count, UNITS), BF16), pltpu.VMEM((2 * count, UNITS), BF16)],
        compiler_params=params(),
        cost_estimate=pl.CostEstimate(flops=4 * UNITS * 2 * count * full, bytes_accessed=12 << 20, transcendentals=0),
        name="outputs_and_feature_grads",
    )(hidden, grad_pre, weights)
    out_peer = to_other_core(out_other)
    out_sum = (out_own.astype(F32) + out_peer.astype(F32)).astype(BF16)
    out_got = exchange(out_sum)
    rows = 128
    outputs, grad_features = pl.pallas_call(
        sums_kernel,
        grid=(count // rows,),
        out_shape=(struct(4, count, part), struct(count, part)),
        in_specs=[pl.BlockSpec((MP, 2, rows, part), lambda t: (0, 0, t, 0))],
        out_specs=(
            pl.BlockSpec((4, rows, part), lambda t: (0, t, 0)),
            pl.BlockSpec((rows, part), lambda t: (t, 0)),
        ),
        compiler_params=params(),
        name="sum_outputs",
    )(out_got)

    left, right = summed[..., :part], summed[..., part:]
    keep = jnp.where(core == 0, left, right)
    give = jnp.where(core == 0, right, left)
    taken = to_other_core(give)
    back = exchange(after(jnp.stack([keep, taken], axis=1), out_got))
    grad_in, grad_out = pl.pallas_call(
        unsort_kernel,
        out_shape=(struct(part, units), struct(units, part)),
        in_specs=[VMEM, VMEM, VMEM],
        out_specs=(VMEM, VMEM),
        compiler_params=params(),
        name="unsort_grads",
    )(places, back[:, 0], back[:, 1])
    return outputs, grad_features, grad_in, grad_out


def solution(mesh):
    whole = Mesh(mesh.devices.reshape(Z, 2, 4, 4), ("z", "core", "y", "x"))
    dp, mp = ("z", "core"), ("y", "x")
    return jax.shard_map(
        per_device,
        mesh=whole,
        in_specs=(P(dp, mp), P(dp, mp), P(mp, dp), P(mp), P(None, dp, mp)),
        out_specs=(P(None, dp, mp), P(dp, mp), P(dp, mp), P(mp, dp)),
        check_vma=False,
    )
```

```python
import functools

import jax
import jax.numpy as jnp
from jax import lax
from jax.experimental import pallas as pl
from jax.experimental.pallas import tpu as pltpu
from jax.sharding import Mesh, PartitionSpec as P

FF = 16384
MP = 16
Z = 8
SHARE = 64
HALF = SHARE // 2
UNITS = MP * HALF
LAST_OF_BAND = (1, 3, 7, 15)

tanh_scale = 0.7978845608
cubic_term = 0.044715

F32 = jnp.float32
BF16 = jnp.bfloat16
MXN = (((1,), (1,)), ((), ()))
TN = (((0,), (0,)), ((), ()))


def params(mib=24):
    return pltpu.CompilerParams(vmem_limit_bytes=mib << 20)


def one_hot(places):
    size = places.shape[1]
    return (lax.broadcasted_iota(jnp.int32, (size, size), 0) == places).astype(BF16)


def sort_kernel(
    core_ref, units_ref, w_in_hbm, w_out_hbm, own_ref, other_ref, places_ref, w_in_ref, w_out_ref, load_sem
):
    loads = [
        pltpu.make_async_copy(w_in_hbm, w_in_ref, load_sem.at[0]),
        pltpu.make_async_copy(w_out_hbm, w_out_ref, load_sem.at[1]),
    ]
    for load in loads:
        load.start()
    units = units_ref[...]
    size = units.shape[1]
    band = (
        (units >= FF // 8).astype(jnp.int32)
        + (units >= FF // 4).astype(jnp.int32)
        + (units >= FF // 2).astype(jnp.int32)
    )
    rows = lax.broadcasted_iota(jnp.int32, (8, size), 0)
    member = rows == band
    before = (
        lax.broadcasted_iota(jnp.int32, (size, size), 0)
        < lax.broadcasted_iota(jnp.int32, (size, size), 1)
    ).astype(BF16)
    count = jnp.dot(member.astype(BF16), before, preferred_element_type=F32)
    base = jnp.where(rows == 0, 0, jnp.where(rows == 1, size // 8, jnp.where(rows == 2, size // 4, size // 2)))
    rank = jnp.sum(jnp.where(member, count + base.astype(F32), 0.0), axis=0, keepdims=True).astype(jnp.int32)
    dest = rank // SHARE
    within = rank % SHARE
    half = within // HALF
    places = jnp.where(half == core_ref[0], 0, UNITS) + dest * HALF + within % HALF
    places_ref[...] = places
    picks = one_hot(places)
    for load in loads:
        load.wait()
    rows_in = lax.dot_general(picks, w_in_ref[...], MXN, preferred_element_type=F32).astype(BF16)
    rows_out = jnp.dot(picks, w_out_ref[...], preferred_element_type=F32).astype(BF16)
    for k in range(MP):
        lo = k * HALF
        own_ref[k, 0] = rows_in[lo : lo + HALF]
        own_ref[k, 1] = rows_out[lo : lo + HALF]
        other_ref[k, 0] = rows_in[UNITS + lo : UNITS + lo + HALF]
        other_ref[k, 1] = rows_out[UNITS + lo : UNITS + lo + HALF]


def unsort_kernel(places_ref, own_ref, other_ref, grad_in_ref, grad_out_ref):
    picks = one_hot(places_ref[...])

    def rows(i):
        return jnp.concatenate([own_ref[k, i] for k in range(MP)] + [other_ref[k, i] for k in range(MP)], axis=0)

    grad_in_ref[...] = lax.dot_general(rows(0), picks, TN, preferred_element_type=F32).astype(BF16)
    grad_out_ref[...] = lax.dot_general(rows(1), picks, TN, preferred_element_type=F32).T.astype(BF16)


def tokens_kernel(x_ref, cot_ref, send_ref):
    x = x_ref[...]
    total = cot_ref[3].astype(F32)
    combined = [None] * 4
    combined[3] = cot_ref[3]
    for b in (2, 1, 0):
        total = total + cot_ref[b].astype(F32)
        combined[b] = total.astype(BF16)
    first = 0
    for b, last in enumerate(LAST_OF_BAND):
        for k in range(first, last + 1):
            send_ref[k, 0] = x
            send_ref[k, 1] = combined[b]
        first = last + 1


def project(left_hidden, left_grad, weights_of, result_ref, target_ref, store_sem):
    part = result_ref.shape[-1]
    stores = []
    for z in range(Z):
        w_in, w_out = weights_of(z)
        for i, (left, right) in enumerate(((left_hidden, w_out), (left_grad, w_in))):
            whole = jnp.dot(left, right, preferred_element_type=F32).astype(BF16)
            for half in range(2):
                result_ref[2 * z + half, i] = whole[:, half * part : (half + 1) * part]
        blocks = pl.ds(2 * z, 2)
        store = pltpu.make_async_copy(result_ref.at[blocks], target_ref.at[blocks], store_sem.at[z])
        store.start()
        stores.append(store)
    return stores


def grads_kernel(
    own_ref, peer_ref, weights_ref, grads_ref, other_ref, hidden_ref, grad_pre_ref,
    x_ref, comb_ref, in_ref, out_ref, part_ref, theirs_ref, hid_ref, gpre_ref,
    token_sem, weight_sem, grad_sem, store_sem, keep_sem,
):
    count = own_ref.shape[1]
    width = weights_ref.shape[-1]
    full = in_ref.shape[-1]
    loads = ([], [])
    for i, (tokens, weights) in enumerate(((x_ref, in_ref), (comb_ref, out_ref))):
        for half, ref in enumerate((own_ref, peer_ref)):
            loads[i].append(
                pltpu.make_async_copy(
                    ref.at[i], tokens.at[pl.ds(half * count, count)], token_sem.at[2 * half + i]
                )
            )
        for z in range(Z):
            loads[i].append(
                pltpu.make_async_copy(
                    weights_ref.at[z, :, i], weights.at[:, :, pl.ds(z * width, width)], weight_sem.at[2 * z + i]
                )
            )
    for load in loads[0] + loads[1]:
        load.start()
    products = []
    for i, (tokens, weights) in enumerate(((x_ref, in_ref), (comb_ref, out_ref))):
        for load in loads[i]:
            load.wait()
        weight = weights[...].reshape(UNITS, full)
        products.append(lax.dot_general(tokens[...], weight, MXN, preferred_element_type=F32))
    pre, back = products
    square = pre * pre
    tangent = jnp.tanh(tanh_scale * (pre + cubic_term * square * pre))
    hid_ref[...] = (0.5 * pre * (1.0 + tangent)).astype(BF16)
    slope = 0.5 * (1.0 + tangent) + 0.5 * pre * (1.0 - tangent * tangent) * tanh_scale * (
        1.0 + 3.0 * cubic_term * square
    )
    gpre_ref[...] = (back * slope).astype(BF16)
    copies = [
        pltpu.make_async_copy(hid_ref.at[pl.ds(0, count)], hidden_ref, keep_sem.at[0]),
        pltpu.make_async_copy(gpre_ref.at[pl.ds(0, count)], grad_pre_ref, keep_sem.at[1]),
    ]
    for copy in copies:
        copy.start()

    def weights_of(z):
        lanes = slice(z * width, (z + 1) * width)
        return [ref[:, :, lanes].reshape(UNITS, width) for ref in (in_ref, out_ref)]

    copies += project(hid_ref[count:], gpre_ref[count:], weights_of, theirs_ref, other_ref, store_sem)
    turned = [left[...].T for left in (gpre_ref, hid_ref)]
    for z in range(Z):
        lanes = slice(z * width, (z + 1) * width)
        for i, tokens in enumerate((x_ref, comb_ref)):
            grad = jnp.dot(turned[i], tokens[:, lanes], preferred_element_type=F32)
            part_ref[z, :, i] = grad.astype(BF16).reshape(MP, HALF, width)
        copy = pltpu.make_async_copy(part_ref.at[z], grads_ref.at[z], grad_sem.at[z])
        copy.start()
        copies.append(copy)
    for copy in copies:
        copy.wait()


def own_kernel(
    hidden_ref, grad_pre_ref, weights_ref, own_ref,
    hid_ref, gpre_ref, held_ref, mine_ref, load_sem, weight_sem, store_sem,
):
    width = weights_ref.shape[-1]
    loads = [
        pltpu.make_async_copy(hidden_ref, hid_ref, load_sem.at[0]),
        pltpu.make_async_copy(grad_pre_ref, gpre_ref, load_sem.at[1]),
    ]
    pieces = [pltpu.make_async_copy(weights_ref.at[z], held_ref.at[z], weight_sem.at[z]) for z in range(Z)]
    for load in loads + pieces:
        load.start()
    for load in loads:
        load.wait()

    def weights_of(z):
        pieces[z].wait()
        return [held_ref[z, :, i].reshape(UNITS, width) for i in range(2)]

    for store in project(hid_ref[...], gpre_ref[...], weights_of, mine_ref, own_ref, store_sem):
        store.wait()


def sums_kernel(got_ref, outputs_ref, dx_ref):
    total = jnp.zeros(dx_ref.shape, F32)
    for k in range(MP):
        total = total + got_ref[k, 0].astype(F32)
        if k in LAST_OF_BAND:
            outputs_ref[LAST_OF_BAND.index(k)] = total.astype(BF16)
    total = jnp.zeros(dx_ref.shape, F32)
    for k in range(MP):
        total = total + got_ref[k, 1].astype(F32)
    dx_ref[...] = total.astype(BF16)


ANY = pl.BlockSpec(memory_space=pl.ANY)
VMEM = pl.BlockSpec(memory_space=pltpu.VMEM)
SMEM = pl.BlockSpec(memory_space=pltpu.SMEM)


def struct(*shape, dtype=BF16):
    return jax.ShapeDtypeStruct(shape, dtype)


def to_other_core(value):
    return lax.ppermute(value, "core", [(0, 1), (1, 0)])


def exchange(value):
    return lax.all_to_all(value, ("y", "x"), 0, 0, tiled=True)


def gate_kernel(*refs):
    del refs


def gate(value, earlier):
    return pl.pallas_call(
        gate_kernel,
        out_shape=struct(*value.shape),
        in_specs=[ANY, ANY],
        out_specs=ANY,
        input_output_aliases={0: 0},
        name="gate",
    )(value, earlier)


def per_device(features, w_in, w_out, unit_order, cotangents):
    core = lax.axis_index("core")
    count, part = features.shape
    units = unit_order.shape[0]
    width = 2 * part
    full = MP * part
    own, other, places = pl.pallas_call(
        sort_kernel,
        out_shape=(
            struct(MP, 2, HALF, part),
            struct(MP, 2, HALF, part),
            struct(1, units, dtype=jnp.int32),
        ),
        in_specs=[SMEM, VMEM, ANY, ANY],
        out_specs=(VMEM, VMEM, VMEM),
        scratch_shapes=[
            pltpu.VMEM(w_in.shape, BF16),
            pltpu.VMEM(w_out.shape, BF16),
            pltpu.SemaphoreType.DMA((2,)),
        ],
        compiler_params=params(),
        name="sort_units",
    )(core.reshape(1), unit_order.reshape(1, units), w_in, w_out)
    got = to_other_core(other)
    both = jnp.where(core == 0, jnp.concatenate([own, got], axis=3), jnp.concatenate([got, own], axis=3))
    mine = exchange(both)
    weights = lax.all_gather(mine.reshape(2 * UNITS, width), "z", axis=0, tiled=True)
    weights = weights.reshape(Z, MP, 2, HALF, width)

    send = pl.pallas_call(
        tokens_kernel,
        out_shape=struct(MP, 2, count, part),
        in_specs=[VMEM, VMEM],
        out_specs=VMEM,
        compiler_params=params(),
        name="combine_cotangents",
    )(features, cotangents)
    tokens = exchange(send)
    tokens = tokens.transpose(1, 2, 0, 3).reshape(2, count, full)
    peer_tokens = to_other_core(tokens)

    grads, out_other, hidden, grad_pre = pl.pallas_call(
        grads_kernel,
        out_shape=(
            struct(Z, MP, 2, HALF, width),
            struct(MP, 2, count, part),
            struct(count, UNITS),
            struct(count, UNITS),
        ),
        in_specs=[ANY] * 3,
        out_specs=(ANY,) * 4,
        scratch_shapes=[
            pltpu.VMEM((2 * count, full), BF16),
            pltpu.VMEM((2 * count, full), BF16),
            pltpu.VMEM((MP, HALF, full), BF16),
            pltpu.VMEM((MP, HALF, full), BF16),
            pltpu.VMEM((Z, MP, 2, HALF, width), BF16),
            pltpu.VMEM((MP, 2, count, part), BF16),
            pltpu.VMEM((2 * count, UNITS), BF16),
            pltpu.VMEM((2 * count, UNITS), BF16),
            pltpu.SemaphoreType.DMA((4,)),
            pltpu.SemaphoreType.DMA((2 * Z,)),
            pltpu.SemaphoreType.DMA((Z,)),
            pltpu.SemaphoreType.DMA((Z,)),
            pltpu.SemaphoreType.DMA((2,)),
        ],
        compiler_params=params(58),
        cost_estimate=pl.CostEstimate(
            flops=10 * UNITS * 2 * count * full, bytes_accessed=20 << 20, transcendentals=UNITS * 2 * count
        ),
        name="hidden_and_weight_grads",
    )(tokens, peer_tokens, weights)
    summed = lax.psum_scatter(grads.reshape(Z * 2 * UNITS, width), "z", scatter_dimension=0, tiled=True)
    summed = summed.reshape(MP, 2, HALF, width)

    out_own = pl.pallas_call(
        own_kernel,
        out_shape=struct(MP, 2, count, part),
        in_specs=[ANY] * 3,
        out_specs=ANY,
        scratch_shapes=[
            pltpu.VMEM((count, UNITS), BF16),
            pltpu.VMEM((count, UNITS), BF16),
            pltpu.VMEM((Z, MP, 2, HALF, width), BF16),
            pltpu.VMEM((MP, 2, count, part), BF16),
            pltpu.SemaphoreType.DMA((2,)),
            pltpu.SemaphoreType.DMA((Z,)),
            pltpu.SemaphoreType.DMA((Z,)),
        ],
        compiler_params=params(50),
        cost_estimate=pl.CostEstimate(flops=4 * UNITS * count * full, bytes_accessed=8 << 20, transcendentals=0),
        name="own_outputs_and_feature_grads",
    )(hidden, grad_pre, weights)
    out_peer = to_other_core(out_other)
    out_sum = (out_own.astype(F32) + out_peer.astype(F32)).astype(BF16)
    out_got = exchange(out_sum)
    rows = 128
    outputs, grad_features = pl.pallas_call(
        sums_kernel,
        grid=(count // rows,),
        out_shape=(struct(4, count, part), struct(count, part)),
        in_specs=[pl.BlockSpec((MP, 2, rows, part), lambda t: (0, 0, t, 0))],
        out_specs=(
            pl.BlockSpec((4, rows, part), lambda t: (0, t, 0)),
            pl.BlockSpec((rows, part), lambda t: (t, 0)),
        ),
        compiler_params=params(),
        name="sum_outputs",
    )(out_got)

    back = exchange(gate(summed, out_got))
    left, right = back[..., :part], back[..., part:]
    keep = jnp.where(core == 0, left, right)
    give = jnp.where(core == 0, right, left)
    grad_in, grad_out = pl.pallas_call(
        unsort_kernel,
        out_shape=(struct(part, units), struct(units, part)),
        in_specs=[VMEM, VMEM, VMEM],
        out_specs=(VMEM, VMEM),
        compiler_params=params(),
        name="unsort_grads",
    )(places, keep, to_other_core(give))
    return outputs, grad_features, grad_in, grad_out


def solution(mesh):
    whole = Mesh(mesh.devices.reshape(Z, 2, 4, 4), ("z", "core", "y", "x"))
    dp, mp = ("z", "core"), ("y", "x")
    return jax.shard_map(
        per_device,
        mesh=whole,
        in_specs=(P(dp, mp), P(dp, mp), P(mp, dp), P(mp), P(None, dp, mp)),
        out_specs=(P(None, dp, mp), P(dp, mp), P(dp, mp), P(mp, dp)),
        check_vma=False,
    )
```

```python
import functools

import jax
import jax.numpy as jnp
from jax import lax
from jax.experimental import pallas as pl
from jax.experimental.pallas import tpu as pltpu
from jax.sharding import Mesh, PartitionSpec as P

FF = 16384
MP = 16
Z = 8
SHARE = 64
HALF = SHARE // 2
UNITS = MP * HALF
LAST_OF_BAND = (1, 3, 7, 15)

tanh_scale = 0.7978845608
cubic_term = 0.044715

F32 = jnp.float32
BF16 = jnp.bfloat16
MXN = (((1,), (1,)), ((), ()))
TN = (((0,), (0,)), ((), ()))


def params(mib=24):
    return pltpu.CompilerParams(vmem_limit_bytes=mib << 20)


def one_hot(places):
    size = places.shape[1]
    return (lax.broadcasted_iota(jnp.int32, (size, size), 0) == places).astype(BF16)


def sort_kernel(
    core_ref, units_hbm, w_in_hbm, w_out_hbm, own_ref, other_ref, places_ref,
    units_ref, w_in_ref, w_out_ref, load_sem,
):
    first, *loads = [
        pltpu.make_async_copy(units_hbm, units_ref, load_sem.at[0]),
        pltpu.make_async_copy(w_in_hbm, w_in_ref, load_sem.at[1]),
        pltpu.make_async_copy(w_out_hbm, w_out_ref, load_sem.at[2]),
    ]
    for load in (first, *loads):
        load.start()
    first.wait()
    units = units_ref[...]
    size = units.shape[1]
    band = (
        (units >= FF // 8).astype(jnp.int32)
        + (units >= FF // 4).astype(jnp.int32)
        + (units >= FF // 2).astype(jnp.int32)
    )
    rows = lax.broadcasted_iota(jnp.int32, (8, size), 0)
    member = rows == band
    before = (
        lax.broadcasted_iota(jnp.int32, (size, size), 0)
        < lax.broadcasted_iota(jnp.int32, (size, size), 1)
    ).astype(BF16)
    count = jnp.dot(member.astype(BF16), before, preferred_element_type=F32)
    base = jnp.where(rows == 0, 0, jnp.where(rows == 1, size // 8, jnp.where(rows == 2, size // 4, size // 2)))
    rank = jnp.sum(jnp.where(member, count + base.astype(F32), 0.0), axis=0, keepdims=True).astype(jnp.int32)
    dest = rank // SHARE
    within = rank % SHARE
    half = within // HALF
    places = jnp.where(half == core_ref[0], 0, UNITS) + dest * HALF + within % HALF
    places_ref[...] = places
    picks = one_hot(places)
    for load in loads:
        load.wait()
    rows_in = lax.dot_general(picks, w_in_ref[...], MXN, preferred_element_type=F32).astype(BF16)
    rows_out = jnp.dot(picks, w_out_ref[...], preferred_element_type=F32).astype(BF16)
    for k in range(MP):
        lo = k * HALF
        own_ref[k, 0] = rows_in[lo : lo + HALF]
        own_ref[k, 1] = rows_out[lo : lo + HALF]
        other_ref[k, 0] = rows_in[UNITS + lo : UNITS + lo + HALF]
        other_ref[k, 1] = rows_out[UNITS + lo : UNITS + lo + HALF]


def unsort_kernel(places_ref, own_ref, other_ref, grad_in_ref, grad_out_ref):
    picks = one_hot(places_ref[...])

    def rows(i):
        return jnp.concatenate([own_ref[k, i] for k in range(MP)] + [other_ref[k, i] for k in range(MP)], axis=0)

    grad_in_ref[...] = lax.dot_general(rows(0), picks, TN, preferred_element_type=F32).astype(BF16)
    grad_out_ref[...] = lax.dot_general(rows(1), picks, TN, preferred_element_type=F32).T.astype(BF16)


def tokens_kernel(x_ref, cot_ref, send_ref):
    x = x_ref[...]
    total = cot_ref[3].astype(F32)
    combined = [None] * 4
    combined[3] = cot_ref[3]
    for b in (2, 1, 0):
        total = total + cot_ref[b].astype(F32)
        combined[b] = total.astype(BF16)
    first = 0
    for b, last in enumerate(LAST_OF_BAND):
        for k in range(first, last + 1):
            send_ref[k, 0] = x
            send_ref[k, 1] = combined[b]
        first = last + 1


def project(left_hidden, left_grad, weights_of, result_ref, target_ref, store_sem):
    part = result_ref.shape[-1]
    stores = []
    for z in range(Z):
        w_in, w_out = weights_of(z)
        for i, (left, right) in enumerate(((left_hidden, w_out), (left_grad, w_in))):
            whole = jnp.dot(left, right, preferred_element_type=F32).astype(BF16)
            for half in range(2):
                result_ref[2 * z + half, i] = whole[:, half * part : (half + 1) * part]
        blocks = pl.ds(2 * z, 2)
        store = pltpu.make_async_copy(result_ref.at[blocks], target_ref.at[blocks], store_sem.at[z])
        store.start()
        stores.append(store)
    return stores


def grads_kernel(
    own_ref, peer_ref, weights_ref, grads_ref, other_ref, hidden_ref, grad_pre_ref,
    x_ref, comb_ref, in_ref, out_ref, part_ref, theirs_ref, hid_ref, gpre_ref,
    token_sem, weight_sem, grad_sem, store_sem, keep_sem,
):
    count = own_ref.shape[1]
    width = weights_ref.shape[-1]
    full = in_ref.shape[-1]
    loads = ([], [])
    for i, (tokens, weights) in enumerate(((x_ref, in_ref), (comb_ref, out_ref))):
        for half, ref in enumerate((own_ref, peer_ref)):
            loads[i].append(
                pltpu.make_async_copy(
                    ref.at[i], tokens.at[pl.ds(half * count, count)], token_sem.at[2 * half + i]
                )
            )
        for z in range(Z):
            loads[i].append(
                pltpu.make_async_copy(
                    weights_ref.at[z, :, i], weights.at[:, :, pl.ds(z * width, width)], weight_sem.at[2 * z + i]
                )
            )
    for load in loads[0] + loads[1]:
        load.start()
    products = []
    for i, (tokens, weights) in enumerate(((x_ref, in_ref), (comb_ref, out_ref))):
        for load in loads[i]:
            load.wait()
        weight = weights[...].reshape(UNITS, full)
        products.append(lax.dot_general(tokens[...], weight, MXN, preferred_element_type=F32))
    pre, back = products
    square = pre * pre
    tangent = jnp.tanh(tanh_scale * (pre + cubic_term * square * pre))
    hid_ref[...] = (0.5 * pre * (1.0 + tangent)).astype(BF16)
    slope = 0.5 * (1.0 + tangent) + 0.5 * pre * (1.0 - tangent * tangent) * tanh_scale * (
        1.0 + 3.0 * cubic_term * square
    )
    gpre_ref[...] = (back * slope).astype(BF16)
    copies = [
        pltpu.make_async_copy(hid_ref.at[pl.ds(0, count)], hidden_ref, keep_sem.at[0]),
        pltpu.make_async_copy(gpre_ref.at[pl.ds(0, count)], grad_pre_ref, keep_sem.at[1]),
    ]
    for copy in copies:
        copy.start()

    def weights_of(z):
        lanes = slice(z * width, (z + 1) * width)
        return [ref[:, :, lanes].reshape(UNITS, width) for ref in (in_ref, out_ref)]

    copies += project(hid_ref[count:], gpre_ref[count:], weights_of, theirs_ref, other_ref, store_sem)
    turned = [left[...].T for left in (gpre_ref, hid_ref)]
    for z in range(Z):
        lanes = slice(z * width, (z + 1) * width)
        for i, tokens in enumerate((x_ref, comb_ref)):
            grad = jnp.dot(turned[i], tokens[:, lanes], preferred_element_type=F32)
            part_ref[z, :, i] = grad.astype(BF16).reshape(MP, HALF, width)
        copy = pltpu.make_async_copy(part_ref.at[z], grads_ref.at[z], grad_sem.at[z])
        copy.start()
        copies.append(copy)
    for copy in copies:
        copy.wait()


def own_kernel(
    hidden_ref, grad_pre_ref, weights_ref, own_ref,
    hid_ref, gpre_ref, held_ref, mine_ref, load_sem, weight_sem, store_sem,
):
    width = weights_ref.shape[-1]
    loads = [
        pltpu.make_async_copy(hidden_ref, hid_ref, load_sem.at[0]),
        pltpu.make_async_copy(grad_pre_ref, gpre_ref, load_sem.at[1]),
    ]
    pieces = [pltpu.make_async_copy(weights_ref.at[z], held_ref.at[z], weight_sem.at[z]) for z in range(Z)]
    for load in loads + pieces:
        load.start()
    for load in loads:
        load.wait()

    def weights_of(z):
        pieces[z].wait()
        return [held_ref[z, :, i].reshape(UNITS, width) for i in range(2)]

    for store in project(hid_ref[...], gpre_ref[...], weights_of, mine_ref, own_ref, store_sem):
        store.wait()


def sums_kernel(got_ref, outputs_ref, dx_ref):
    total = jnp.zeros(dx_ref.shape, F32)
    for k in range(MP):
        total = total + got_ref[k, 0].astype(F32)
        if k in LAST_OF_BAND:
            outputs_ref[LAST_OF_BAND.index(k)] = total.astype(BF16)
    total = jnp.zeros(dx_ref.shape, F32)
    for k in range(MP):
        total = total + got_ref[k, 1].astype(F32)
    dx_ref[...] = total.astype(BF16)


ANY = pl.BlockSpec(memory_space=pl.ANY)
VMEM = pl.BlockSpec(memory_space=pltpu.VMEM)
SMEM = pl.BlockSpec(memory_space=pltpu.SMEM)


def struct(*shape, dtype=BF16):
    return jax.ShapeDtypeStruct(shape, dtype)


def in_hbm(value):
    return pltpu.with_memory_space_constraint(value, pltpu.HBM)


def to_other_core(value):
    return lax.ppermute(value, "core", [(0, 1), (1, 0)])


def exchange(value):
    return lax.all_to_all(value, ("y", "x"), 0, 0, tiled=True)


def gate_kernel(*refs):
    del refs


def gate(value, earlier):
    return pl.pallas_call(
        gate_kernel,
        out_shape=struct(*value.shape),
        in_specs=[ANY, ANY],
        out_specs=ANY,
        input_output_aliases={0: 0},
        name="gate",
    )(in_hbm(value), earlier)


def per_device(features, w_in, w_out, unit_order, cotangents):
    core = lax.axis_index("core")
    count, part = features.shape
    units = unit_order.shape[0]
    width = 2 * part
    full = MP * part
    own, other, places = pl.pallas_call(
        sort_kernel,
        out_shape=(
            struct(MP, 2, HALF, part),
            struct(MP, 2, HALF, part),
            struct(1, units, dtype=jnp.int32),
        ),
        in_specs=[SMEM, ANY, ANY, ANY],
        out_specs=(VMEM, VMEM, VMEM),
        scratch_shapes=[
            pltpu.VMEM((1, units), jnp.int32),
            pltpu.VMEM(w_in.shape, BF16),
            pltpu.VMEM(w_out.shape, BF16),
            pltpu.SemaphoreType.DMA((3,)),
        ],
        compiler_params=params(),
        name="sort_units",
    )(core.reshape(1), *map(in_hbm, (unit_order.reshape(1, units), w_in, w_out)))
    got = to_other_core(other)
    both = jnp.where(core == 0, jnp.concatenate([own, got], axis=3), jnp.concatenate([got, own], axis=3))
    mine = exchange(both)
    weights = lax.all_gather(mine.reshape(2 * UNITS, width), "z", axis=0, tiled=True)
    weights = weights.reshape(Z, MP, 2, HALF, width)

    send = pl.pallas_call(
        tokens_kernel,
        out_shape=struct(MP, 2, count, part),
        in_specs=[VMEM, VMEM],
        out_specs=VMEM,
        compiler_params=params(),
        name="combine_cotangents",
    )(features, cotangents)
    tokens = exchange(send)
    tokens = tokens.transpose(1, 2, 0, 3).reshape(2, count, full)
    peer_tokens = to_other_core(tokens)

    grads, out_other, hidden, grad_pre = pl.pallas_call(
        grads_kernel,
        out_shape=(
            struct(Z, MP, 2, HALF, width),
            struct(MP, 2, count, part),
            struct(count, UNITS),
            struct(count, UNITS),
        ),
        in_specs=[ANY] * 3,
        out_specs=(ANY,) * 4,
        scratch_shapes=[
            pltpu.VMEM((2 * count, full), BF16),
            pltpu.VMEM((2 * count, full), BF16),
            pltpu.VMEM((MP, HALF, full), BF16),
            pltpu.VMEM((MP, HALF, full), BF16),
            pltpu.VMEM((Z, MP, 2, HALF, width), BF16),
            pltpu.VMEM((MP, 2, count, part), BF16),
            pltpu.VMEM((2 * count, UNITS), BF16),
            pltpu.VMEM((2 * count, UNITS), BF16),
            pltpu.SemaphoreType.DMA((4,)),
            pltpu.SemaphoreType.DMA((2 * Z,)),
            pltpu.SemaphoreType.DMA((Z,)),
            pltpu.SemaphoreType.DMA((Z,)),
            pltpu.SemaphoreType.DMA((2,)),
        ],
        compiler_params=params(58),
        cost_estimate=pl.CostEstimate(
            flops=10 * UNITS * 2 * count * full, bytes_accessed=20 << 20, transcendentals=UNITS * 2 * count
        ),
        name="hidden_and_weight_grads",
    )(tokens, peer_tokens, weights)
    summed = lax.psum_scatter(grads.reshape(Z * 2 * UNITS, width), "z", scatter_dimension=0, tiled=True)
    summed = summed.reshape(MP, 2, HALF, width)

    out_own = pl.pallas_call(
        own_kernel,
        out_shape=struct(MP, 2, count, part),
        in_specs=[ANY] * 3,
        out_specs=ANY,
        scratch_shapes=[
            pltpu.VMEM((count, UNITS), BF16),
            pltpu.VMEM((count, UNITS), BF16),
            pltpu.VMEM((Z, MP, 2, HALF, width), BF16),
            pltpu.VMEM((MP, 2, count, part), BF16),
            pltpu.SemaphoreType.DMA((2,)),
            pltpu.SemaphoreType.DMA((Z,)),
            pltpu.SemaphoreType.DMA((Z,)),
        ],
        compiler_params=params(50),
        cost_estimate=pl.CostEstimate(flops=4 * UNITS * count * full, bytes_accessed=8 << 20, transcendentals=0),
        name="own_outputs_and_feature_grads",
    )(*map(in_hbm, (hidden, grad_pre, weights)))
    out_peer = to_other_core(out_other)
    out_sum = (out_own.astype(F32) + out_peer.astype(F32)).astype(BF16)
    out_got = exchange(out_sum)
    rows = 128
    outputs, grad_features = pl.pallas_call(
        sums_kernel,
        grid=(count // rows,),
        out_shape=(struct(4, count, part), struct(count, part)),
        in_specs=[pl.BlockSpec((MP, 2, rows, part), lambda t: (0, 0, t, 0))],
        out_specs=(
            pl.BlockSpec((4, rows, part), lambda t: (0, t, 0)),
            pl.BlockSpec((rows, part), lambda t: (t, 0)),
        ),
        compiler_params=params(),
        name="sum_outputs",
    )(out_got)

    back = exchange(gate(summed, out_got))
    left, right = back[..., :part], back[..., part:]
    keep = jnp.where(core == 0, left, right)
    give = jnp.where(core == 0, right, left)
    grad_in, grad_out = pl.pallas_call(
        unsort_kernel,
        out_shape=(struct(part, units), struct(units, part)),
        in_specs=[VMEM, VMEM, VMEM],
        out_specs=(VMEM, VMEM),
        compiler_params=params(),
        name="unsort_grads",
    )(places, keep, to_other_core(give))
    return outputs, grad_features, grad_in, grad_out


def solution(mesh):
    whole = Mesh(mesh.devices.reshape(Z, 2, 4, 4), ("z", "core", "y", "x"))
    dp, mp = ("z", "core"), ("y", "x")
    return jax.shard_map(
        per_device,
        mesh=whole,
        in_specs=(P(dp, mp), P(dp, mp), P(mp, dp), P(mp), P(None, dp, mp)),
        out_specs=(P(None, dp, mp), P(dp, mp), P(dp, mp), P(mp, dp)),
        check_vma=False,
    )
```

```python
import functools

import jax
import jax.numpy as jnp
from jax import lax
from jax.experimental import pallas as pl
from jax.experimental.pallas import tpu as pltpu
from jax.sharding import Mesh, PartitionSpec as P

FF = 16384
MP = 16
Z = 8
SHARE = 64
HALF = SHARE // 2
UNITS = MP * HALF
LAST_OF_BAND = (1, 3, 7, 15)

tanh_scale = 0.7978845608
cubic_term = 0.044715

F32 = jnp.float32
BF16 = jnp.bfloat16
MXN = (((1,), (1,)), ((), ()))
TN = (((0,), (0,)), ((), ()))


def params(mib=24):
    return pltpu.CompilerParams(vmem_limit_bytes=mib << 20)


def one_hot(places):
    size = places.shape[1]
    return (lax.broadcasted_iota(jnp.int32, (size, size), 0) == places).astype(BF16)


def sort_kernel(
    core_ref, units_hbm, w_in_hbm, w_out_hbm, own_ref, other_ref, places_ref,
    units_ref, w_in_ref, w_out_ref, load_sem,
):
    first, *loads = [
        pltpu.make_async_copy(units_hbm, units_ref, load_sem.at[0]),
        pltpu.make_async_copy(w_in_hbm, w_in_ref, load_sem.at[1]),
        pltpu.make_async_copy(w_out_hbm, w_out_ref, load_sem.at[2]),
    ]
    for load in (first, *loads):
        load.start()
    first.wait()
    units = units_ref[...]
    size = units.shape[1]
    band = (
        (units >= FF // 8).astype(jnp.int32)
        + (units >= FF // 4).astype(jnp.int32)
        + (units >= FF // 2).astype(jnp.int32)
    )
    rows = lax.broadcasted_iota(jnp.int32, (8, size), 0)
    member = rows == band
    before = (
        lax.broadcasted_iota(jnp.int32, (size, size), 0)
        < lax.broadcasted_iota(jnp.int32, (size, size), 1)
    ).astype(BF16)
    count = jnp.dot(member.astype(BF16), before, preferred_element_type=F32)
    base = jnp.where(rows == 0, 0, jnp.where(rows == 1, size // 8, jnp.where(rows == 2, size // 4, size // 2)))
    rank = jnp.sum(jnp.where(member, count + base.astype(F32), 0.0), axis=0, keepdims=True).astype(jnp.int32)
    dest = rank // SHARE
    within = rank % SHARE
    half = within // HALF
    places = jnp.where(half == core_ref[0], 0, UNITS) + dest * HALF + within % HALF
    places_ref[...] = places
    picks = one_hot(places)
    for load in loads:
        load.wait()
    rows_in = lax.dot_general(picks, w_in_ref[...], MXN, preferred_element_type=F32).astype(BF16)
    rows_out = jnp.dot(picks, w_out_ref[...], preferred_element_type=F32).astype(BF16)
    for k in range(MP):
        lo = k * HALF
        own_ref[k, 0] = rows_in[lo : lo + HALF]
        own_ref[k, 1] = rows_out[lo : lo + HALF]
        other_ref[k, 0] = rows_in[UNITS + lo : UNITS + lo + HALF]
        other_ref[k, 1] = rows_out[UNITS + lo : UNITS + lo + HALF]


def unsort_kernel(places_ref, own_ref, other_ref, grad_in_ref, grad_out_ref):
    picks = one_hot(places_ref[...])

    def rows(i):
        return jnp.concatenate([own_ref[k, i] for k in range(MP)] + [other_ref[k, i] for k in range(MP)], axis=0)

    grad_in_ref[...] = lax.dot_general(rows(0), picks, TN, preferred_element_type=F32).astype(BF16)
    grad_out_ref[...] = lax.dot_general(rows(1), picks, TN, preferred_element_type=F32).T.astype(BF16)


def tokens_kernel(x_ref, cot_ref, send_ref):
    x = x_ref[...]
    total = cot_ref[3].astype(F32)
    combined = [None] * 4
    combined[3] = cot_ref[3]
    for b in (2, 1, 0):
        total = total + cot_ref[b].astype(F32)
        combined[b] = total.astype(BF16)
    first = 0
    for b, last in enumerate(LAST_OF_BAND):
        for k in range(first, last + 1):
            send_ref[k, 0] = x
            send_ref[k, 1] = combined[b]
        first = last + 1


def project(left_hidden, left_grad, weights_of, result_ref, target_ref, store_sem):
    part = result_ref.shape[-1]
    stores = []
    for z in range(Z):
        w_in, w_out = weights_of(z)
        for i, (left, right) in enumerate(((left_hidden, w_out), (left_grad, w_in))):
            whole = jnp.dot(left, right, preferred_element_type=F32).astype(BF16)
            for half in range(2):
                result_ref[2 * z + half, i] = whole[:, half * part : (half + 1) * part]
        blocks = pl.ds(2 * z, 2)
        store = pltpu.make_async_copy(result_ref.at[blocks], target_ref.at[blocks], store_sem.at[z])
        store.start()
        stores.append(store)
    return stores


def grads_kernel(
    own_ref, peer_ref, weights_ref, grads_ref, other_ref, hidden_ref, grad_pre_ref,
    x_ref, comb_ref, in_ref, out_ref, part_ref, theirs_ref, hid_ref, gpre_ref,
    token_sem, weight_sem, grad_sem, store_sem, keep_sem,
):
    count = own_ref.shape[1]
    width = weights_ref.shape[-1]
    full = in_ref.shape[-1]
    loads = ([], [])
    for i, (tokens, weights) in enumerate(((x_ref, in_ref), (comb_ref, out_ref))):
        for half, ref in enumerate((own_ref, peer_ref)):
            loads[i].append(
                pltpu.make_async_copy(
                    ref.at[i], tokens.at[pl.ds(half * count, count)], token_sem.at[2 * half + i]
                )
            )
        for z in range(Z):
            loads[i].append(
                pltpu.make_async_copy(
                    weights_ref.at[z, :, i], weights.at[:, :, pl.ds(z * width, width)], weight_sem.at[2 * z + i]
                )
            )
    for load in loads[0] + loads[1]:
        load.start()
    products = []
    for i, (tokens, weights) in enumerate(((x_ref, in_ref), (comb_ref, out_ref))):
        for load in loads[i]:
            load.wait()
        weight = weights[...].reshape(UNITS, full)
        products.append(lax.dot_general(tokens[...], weight, MXN, preferred_element_type=F32))
    pre, back = products
    square = pre * pre
    tangent = jnp.tanh(tanh_scale * (pre + cubic_term * square * pre))
    hid_ref[...] = (0.5 * pre * (1.0 + tangent)).astype(BF16)
    slope = 0.5 * (1.0 + tangent) + 0.5 * pre * (1.0 - tangent * tangent) * tanh_scale * (
        1.0 + 3.0 * cubic_term * square
    )
    gpre_ref[...] = (back * slope).astype(BF16)
    copies = [
        pltpu.make_async_copy(hid_ref.at[pl.ds(0, count)], hidden_ref, keep_sem.at[0]),
        pltpu.make_async_copy(gpre_ref.at[pl.ds(0, count)], grad_pre_ref, keep_sem.at[1]),
    ]
    for copy in copies:
        copy.start()

    def weights_of(z):
        lanes = slice(z * width, (z + 1) * width)
        return [ref[:, :, lanes].reshape(UNITS, width) for ref in (in_ref, out_ref)]

    copies += project(hid_ref[count:], gpre_ref[count:], weights_of, theirs_ref, other_ref, store_sem)
    turned = [left[...].T for left in (gpre_ref, hid_ref)]
    for z in range(Z):
        lanes = slice(z * width, (z + 1) * width)
        for i, tokens in enumerate((x_ref, comb_ref)):
            grad = jnp.dot(turned[i], tokens[:, lanes], preferred_element_type=F32)
            part_ref[z, :, i] = grad.astype(BF16).reshape(MP, HALF, width)
        copy = pltpu.make_async_copy(part_ref.at[z], grads_ref.at[z], grad_sem.at[z])
        copy.start()
        copies.append(copy)
    for copy in copies:
        copy.wait()


def own_kernel(
    hidden_ref, grad_pre_ref, weights_ref, own_ref,
    hid_ref, gpre_ref, held_ref, mine_ref, load_sem, weight_sem, store_sem,
):
    width = weights_ref.shape[-1]
    loads = [
        pltpu.make_async_copy(hidden_ref, hid_ref, load_sem.at[0]),
        pltpu.make_async_copy(grad_pre_ref, gpre_ref, load_sem.at[1]),
    ]
    pieces = [pltpu.make_async_copy(weights_ref.at[z], held_ref.at[z], weight_sem.at[z]) for z in range(Z)]
    for load in loads + pieces:
        load.start()
    for load in loads:
        load.wait()

    def weights_of(z):
        pieces[z].wait()
        return [held_ref[z, :, i].reshape(UNITS, width) for i in range(2)]

    for store in project(hid_ref[...], gpre_ref[...], weights_of, mine_ref, own_ref, store_sem):
        store.wait()


def sums_kernel(got_ref, outputs_ref, dx_ref):
    total = jnp.zeros(dx_ref.shape, F32)
    for k in range(MP):
        total = total + got_ref[k, 0].astype(F32)
        if k in LAST_OF_BAND:
            outputs_ref[LAST_OF_BAND.index(k)] = total.astype(BF16)
    total = jnp.zeros(dx_ref.shape, F32)
    for k in range(MP):
        total = total + got_ref[k, 1].astype(F32)
    dx_ref[...] = total.astype(BF16)


ANY = pl.BlockSpec(memory_space=pl.ANY)
VMEM = pl.BlockSpec(memory_space=pltpu.VMEM)
SMEM = pl.BlockSpec(memory_space=pltpu.SMEM)


def struct(*shape, dtype=BF16):
    return jax.ShapeDtypeStruct(shape, dtype)


def in_hbm(value):
    return pltpu.with_memory_space_constraint(value, pltpu.HBM)


def to_other_core(value):
    return lax.ppermute(value, "core", [(0, 1), (1, 0)])


def exchange(value):
    return lax.all_to_all(value, ("y", "x"), 0, 0, tiled=True)


def gate_kernel(*refs):
    del refs


def gate(value, earlier):
    return pl.pallas_call(
        gate_kernel,
        out_shape=struct(*value.shape),
        in_specs=[ANY, ANY],
        out_specs=ANY,
        input_output_aliases={0: 0},
        name="gate",
    )(in_hbm(value), earlier)


def per_device(features, w_in, w_out, unit_order, cotangents):
    core = lax.axis_index("core")
    count, part = features.shape
    units = unit_order.shape[0]
    width = 2 * part
    full = MP * part
    own, other, places = pl.pallas_call(
        sort_kernel,
        out_shape=(
            struct(MP, 2, HALF, part),
            struct(MP, 2, HALF, part),
            struct(1, units, dtype=jnp.int32),
        ),
        in_specs=[SMEM, ANY, ANY, ANY],
        out_specs=(VMEM, VMEM, VMEM),
        scratch_shapes=[
            pltpu.VMEM((1, units), jnp.int32),
            pltpu.VMEM(w_in.shape, BF16),
            pltpu.VMEM(w_out.shape, BF16),
            pltpu.SemaphoreType.DMA((3,)),
        ],
        compiler_params=params(),
        name="sort_units",
    )(core.reshape(1), *map(in_hbm, (unit_order.reshape(1, units), w_in, w_out)))
    got = to_other_core(other)
    both = jnp.where(core == 0, jnp.concatenate([own, got], axis=3), jnp.concatenate([got, own], axis=3))
    mine = exchange(both)
    weights = lax.all_gather(mine.reshape(2 * UNITS, width), "z", axis=0, tiled=True)
    weights = weights.reshape(Z, MP, 2, HALF, width)

    send = pl.pallas_call(
        tokens_kernel,
        out_shape=struct(MP, 2, count, part),
        in_specs=[VMEM, VMEM],
        out_specs=VMEM,
        compiler_params=params(),
        name="combine_cotangents",
    )(features, cotangents)
    tokens = exchange(send)
    tokens = tokens.transpose(1, 2, 0, 3).reshape(2, count, full)
    peer_tokens = to_other_core(tokens)

    grads, out_other, hidden, grad_pre = pl.pallas_call(
        grads_kernel,
        out_shape=(
            struct(Z, MP, 2, HALF, width),
            struct(MP, 2, count, part),
            struct(count, UNITS),
            struct(count, UNITS),
        ),
        in_specs=[ANY] * 3,
        out_specs=(ANY,) * 4,
        scratch_shapes=[
            pltpu.VMEM((2 * count, full), BF16),
            pltpu.VMEM((2 * count, full), BF16),
            pltpu.VMEM((MP, HALF, full), BF16),
            pltpu.VMEM((MP, HALF, full), BF16),
            pltpu.VMEM((Z, MP, 2, HALF, width), BF16),
            pltpu.VMEM((MP, 2, count, part), BF16),
            pltpu.VMEM((2 * count, UNITS), BF16),
            pltpu.VMEM((2 * count, UNITS), BF16),
            pltpu.SemaphoreType.DMA((4,)),
            pltpu.SemaphoreType.DMA((2 * Z,)),
            pltpu.SemaphoreType.DMA((Z,)),
            pltpu.SemaphoreType.DMA((Z,)),
            pltpu.SemaphoreType.DMA((2,)),
        ],
        compiler_params=params(58),
        cost_estimate=pl.CostEstimate(
            flops=10 * UNITS * 2 * count * full, bytes_accessed=20 << 20, transcendentals=UNITS * 2 * count
        ),
        name="hidden_and_weight_grads",
    )(tokens, peer_tokens, weights)
    summed = lax.psum_scatter(grads.reshape(Z * 2 * UNITS, width), "z", scatter_dimension=0, tiled=True)
    summed = summed.reshape(MP, 2, HALF, width)

    out_own = pl.pallas_call(
        own_kernel,
        out_shape=struct(MP, 2, count, part),
        in_specs=[ANY] * 3,
        out_specs=ANY,
        scratch_shapes=[
            pltpu.VMEM((count, UNITS), BF16),
            pltpu.VMEM((count, UNITS), BF16),
            pltpu.VMEM((Z, MP, 2, HALF, width), BF16),
            pltpu.VMEM((MP, 2, count, part), BF16),
            pltpu.SemaphoreType.DMA((2,)),
            pltpu.SemaphoreType.DMA((Z,)),
            pltpu.SemaphoreType.DMA((Z,)),
        ],
        compiler_params=params(50),
        cost_estimate=pl.CostEstimate(flops=4 * UNITS * count * full, bytes_accessed=8 << 20, transcendentals=0),
        name="own_outputs_and_feature_grads",
    )(hidden, grad_pre, weights)
    out_peer = to_other_core(out_other)
    out_sum = (out_own.astype(F32) + out_peer.astype(F32)).astype(BF16)
    out_got = exchange(out_sum)
    rows = 128
    outputs, grad_features = pl.pallas_call(
        sums_kernel,
        grid=(count // rows,),
        out_shape=(struct(4, count, part), struct(count, part)),
        in_specs=[pl.BlockSpec((MP, 2, rows, part), lambda t: (0, 0, t, 0))],
        out_specs=(
            pl.BlockSpec((4, rows, part), lambda t: (0, t, 0)),
            pl.BlockSpec((rows, part), lambda t: (t, 0)),
        ),
        compiler_params=params(),
        name="sum_outputs",
    )(out_got)

    back = exchange(gate(summed, out_got))
    left, right = back[..., :part], back[..., part:]
    keep = jnp.where(core == 0, left, right)
    give = jnp.where(core == 0, right, left)
    grad_in, grad_out = pl.pallas_call(
        unsort_kernel,
        out_shape=(struct(part, units), struct(units, part)),
        in_specs=[VMEM, VMEM, VMEM],
        out_specs=(VMEM, VMEM),
        compiler_params=params(),
        name="unsort_grads",
    )(places, keep, to_other_core(give))
    return outputs, grad_features, grad_in, grad_out


def solution(mesh):
    whole = Mesh(mesh.devices.reshape(Z, 2, 4, 4), ("z", "core", "y", "x"))
    dp, mp = ("z", "core"), ("y", "x")
    return jax.shard_map(
        per_device,
        mesh=whole,
        in_specs=(P(dp, mp), P(dp, mp), P(mp, dp), P(mp), P(None, dp, mp)),
        out_specs=(P(None, dp, mp), P(dp, mp), P(dp, mp), P(mp, dp)),
        check_vma=False,
    )
```

```python
import functools

import jax
import jax.numpy as jnp
from jax import lax
from jax.experimental import pallas as pl
from jax.experimental.pallas import tpu as pltpu
from jax.sharding import Mesh, PartitionSpec as P

FF = 16384
MP = 16
Z = 8
SHARE = 64
HALF = SHARE // 2
UNITS = MP * HALF
LAST_OF_BAND = (1, 3, 7, 15)

tanh_scale = 0.7978845608
cubic_term = 0.044715

F32 = jnp.float32
BF16 = jnp.bfloat16
MXN = (((1,), (1,)), ((), ()))
TN = (((0,), (0,)), ((), ()))


def params(mib=24):
    return pltpu.CompilerParams(vmem_limit_bytes=mib << 20)


def one_hot(places):
    rows, lanes = places.shape
    number = lax.broadcasted_iota(jnp.int32, (rows * lanes, lanes), 0)
    return jnp.concatenate([(number == places[r : r + 1]).astype(BF16) for r in range(rows)], axis=1)


def sort_kernel(
    core_ref, units_hbm, w_in_hbm, w_out_hbm, own_ref, other_ref, places_ref,
    units_ref, w_in_ref, w_out_ref, load_sem,
):
    first, *loads = [
        pltpu.make_async_copy(units_hbm, units_ref, load_sem.at[0]),
        pltpu.make_async_copy(w_in_hbm, w_in_ref, load_sem.at[1]),
        pltpu.make_async_copy(w_out_hbm, w_out_ref, load_sem.at[2]),
    ]
    for load in (first, *loads):
        load.start()
    first.wait()
    units = units_ref[...]
    band = (
        (units >= FF // 8).astype(jnp.int32)
        + (units >= FF // 4).astype(jnp.int32)
        + (units >= FF // 2).astype(jnp.int32)
    )
    count, lanes = band.shape
    members = [band == b for b in range(4)]
    stacked = jnp.concatenate([member.astype(F32) for member in members], axis=0)
    before = (
        lax.broadcasted_iota(jnp.int32, (lanes, lanes), 0) < lax.broadcasted_iota(jnp.int32, (lanes, lanes), 1)
    ).astype(BF16)
    within_row = jnp.dot(stacked.astype(BF16), before, preferred_element_type=F32)
    totals = jnp.sum(stacked, axis=1, keepdims=True)
    size = count * lanes
    ranks = [jnp.zeros((1, lanes), F32)] * count
    for b, base in enumerate((0, size // 8, size // 4, size // 2)):
        so_far = jnp.full((1, 1), base, F32)
        for r in range(count):
            row = slice(b * count + r, b * count + r + 1)
            ranks[r] = ranks[r] + stacked[row] * (within_row[row] + so_far)
            so_far = so_far + totals[row]
    rank = jnp.concatenate(ranks, axis=0).astype(jnp.int32)
    dest = rank // SHARE
    within = rank % SHARE
    half = within // HALF
    places = jnp.where(half == core_ref[0], 0, UNITS) + dest * HALF + within % HALF
    places_ref[...] = places
    picks = one_hot(places)
    for load in loads:
        load.wait()
    rows_in = lax.dot_general(picks, w_in_ref[...], MXN, preferred_element_type=F32).astype(BF16)
    rows_out = jnp.dot(picks, w_out_ref[...], preferred_element_type=F32).astype(BF16)
    for k in range(MP):
        lo = k * HALF
        own_ref[k, 0] = rows_in[lo : lo + HALF]
        own_ref[k, 1] = rows_out[lo : lo + HALF]
        other_ref[k, 0] = rows_in[UNITS + lo : UNITS + lo + HALF]
        other_ref[k, 1] = rows_out[UNITS + lo : UNITS + lo + HALF]


def unsort_kernel(places_ref, own_ref, other_ref, grad_in_ref, grad_out_ref):
    picks = one_hot(places_ref[...])

    def rows(i):
        return jnp.concatenate([own_ref[k, i] for k in range(MP)] + [other_ref[k, i] for k in range(MP)], axis=0)

    grad_in_ref[...] = lax.dot_general(rows(0), picks, TN, preferred_element_type=F32).astype(BF16)
    grad_out_ref[...] = lax.dot_general(rows(1), picks, TN, preferred_element_type=F32).T.astype(BF16)


def tokens_kernel(x_ref, cot_ref, send_ref):
    x = x_ref[...]
    total = cot_ref[3].astype(F32)
    combined = [None] * 4
    combined[3] = cot_ref[3]
    for b in (2, 1, 0):
        total = total + cot_ref[b].astype(F32)
        combined[b] = total.astype(BF16)
    first = 0
    for b, last in enumerate(LAST_OF_BAND):
        for k in range(first, last + 1):
            send_ref[k, 0] = x
            send_ref[k, 1] = combined[b]
        first = last + 1


def project(left_hidden, left_grad, weights_of, result_ref, target_ref, store_sem):
    part = result_ref.shape[-1]
    stores = []
    for z in range(Z):
        w_in, w_out = weights_of(z)
        for i, (left, right) in enumerate(((left_hidden, w_out), (left_grad, w_in))):
            whole = jnp.dot(left, right, preferred_element_type=F32).astype(BF16)
            for half in range(2):
                result_ref[2 * z + half, i] = whole[:, half * part : (half + 1) * part]
        blocks = pl.ds(2 * z, 2)
        store = pltpu.make_async_copy(result_ref.at[blocks], target_ref.at[blocks], store_sem.at[z])
        store.start()
        stores.append(store)
    return stores


def grads_kernel(
    own_ref, peer_ref, weights_ref, grads_ref, other_ref, hidden_ref, grad_pre_ref,
    x_ref, comb_ref, in_ref, out_ref, part_ref, theirs_ref, hid_ref, gpre_ref,
    token_sem, weight_sem, grad_sem, store_sem, keep_sem,
):
    count = own_ref.shape[1]
    width = weights_ref.shape[-1]
    full = in_ref.shape[-1]
    loads = ([], [])
    for i, (tokens, weights) in enumerate(((x_ref, in_ref), (comb_ref, out_ref))):
        for half, ref in enumerate((own_ref, peer_ref)):
            loads[i].append(
                pltpu.make_async_copy(
                    ref.at[i], tokens.at[pl.ds(half * count, count)], token_sem.at[2 * half + i]
                )
            )
        for z in range(Z):
            loads[i].append(
                pltpu.make_async_copy(
                    weights_ref.at[z, :, i], weights.at[:, :, pl.ds(z * width, width)], weight_sem.at[2 * z + i]
                )
            )
    for load in loads[0] + loads[1]:
        load.start()
    products = []
    for i, (tokens, weights) in enumerate(((x_ref, in_ref), (comb_ref, out_ref))):
        for load in loads[i]:
            load.wait()
        weight = weights[...].reshape(UNITS, full)
        products.append(lax.dot_general(tokens[...], weight, MXN, preferred_element_type=F32))
    pre, back = products
    square = pre * pre
    tangent = jnp.tanh(tanh_scale * (pre + cubic_term * square * pre))
    hid_ref[...] = (0.5 * pre * (1.0 + tangent)).astype(BF16)
    slope = 0.5 * (1.0 + tangent) + 0.5 * pre * (1.0 - tangent * tangent) * tanh_scale * (
        1.0 + 3.0 * cubic_term * square
    )
    gpre_ref[...] = (back * slope).astype(BF16)
    copies = [
        pltpu.make_async_copy(hid_ref.at[pl.ds(0, count)], hidden_ref, keep_sem.at[0]),
        pltpu.make_async_copy(gpre_ref.at[pl.ds(0, count)], grad_pre_ref, keep_sem.at[1]),
    ]
    for copy in copies:
        copy.start()

    def weights_of(z):
        lanes = slice(z * width, (z + 1) * width)
        return [ref[:, :, lanes].reshape(UNITS, width) for ref in (in_ref, out_ref)]

    copies += project(hid_ref[count:], gpre_ref[count:], weights_of, theirs_ref, other_ref, store_sem)
    turned = [left[...].T for left in (gpre_ref, hid_ref)]
    for z in range(Z):
        lanes = slice(z * width, (z + 1) * width)
        for i, tokens in enumerate((x_ref, comb_ref)):
            grad = jnp.dot(turned[i], tokens[:, lanes], preferred_element_type=F32)
            part_ref[z, :, i] = grad.astype(BF16).reshape(MP, HALF, width)
        copy = pltpu.make_async_copy(part_ref.at[z], grads_ref.at[z], grad_sem.at[z])
        copy.start()
        copies.append(copy)
    for copy in copies:
        copy.wait()


def own_kernel(
    hidden_ref, grad_pre_ref, weights_ref, own_ref,
    hid_ref, gpre_ref, held_ref, mine_ref, load_sem, weight_sem, store_sem,
):
    width = weights_ref.shape[-1]
    loads = [
        pltpu.make_async_copy(hidden_ref, hid_ref, load_sem.at[0]),
        pltpu.make_async_copy(grad_pre_ref, gpre_ref, load_sem.at[1]),
    ]
    pieces = [pltpu.make_async_copy(weights_ref.at[z], held_ref.at[z], weight_sem.at[z]) for z in range(Z)]
    for load in loads + pieces:
        load.start()
    for load in loads:
        load.wait()

    def weights_of(z):
        pieces[z].wait()
        return [held_ref[z, :, i].reshape(UNITS, width) for i in range(2)]

    for store in project(hid_ref[...], gpre_ref[...], weights_of, mine_ref, own_ref, store_sem):
        store.wait()


def sums_kernel(got_ref, outputs_ref, dx_ref):
    total = jnp.zeros(dx_ref.shape, F32)
    for k in range(MP):
        total = total + got_ref[k, 0].astype(F32)
        if k in LAST_OF_BAND:
            outputs_ref[LAST_OF_BAND.index(k)] = total.astype(BF16)
    total = jnp.zeros(dx_ref.shape, F32)
    for k in range(MP):
        total = total + got_ref[k, 1].astype(F32)
    dx_ref[...] = total.astype(BF16)


ANY = pl.BlockSpec(memory_space=pl.ANY)
VMEM = pl.BlockSpec(memory_space=pltpu.VMEM)
SMEM = pl.BlockSpec(memory_space=pltpu.SMEM)


def struct(*shape, dtype=BF16):
    return jax.ShapeDtypeStruct(shape, dtype)


def in_hbm(value):
    return pltpu.with_memory_space_constraint(value, pltpu.HBM)


def in_vmem(value):
    return pltpu.with_memory_space_constraint(value, pltpu.VMEM)


def to_other_core(value):
    return lax.ppermute(value, "core", [(0, 1), (1, 0)])


def exchange(value):
    return lax.all_to_all(value, ("y", "x"), 0, 0, tiled=True)


def gate_kernel(*refs):
    del refs


def gate(value, earlier):
    return pl.pallas_call(
        gate_kernel,
        out_shape=struct(*value.shape),
        in_specs=[ANY, ANY],
        out_specs=ANY,
        input_output_aliases={0: 0},
        name="gate",
    )(in_hbm(value), earlier)


def per_device(features, w_in, w_out, unit_order, cotangents):
    core = lax.axis_index("core")
    count, part = features.shape
    units = unit_order.shape[0]
    width = 2 * part
    full = MP * part
    own, other, places = pl.pallas_call(
        sort_kernel,
        out_shape=(
            struct(MP, 2, HALF, part),
            struct(MP, 2, HALF, part),
            struct(units // part, part, dtype=jnp.int32),
        ),
        in_specs=[SMEM, ANY, ANY, ANY],
        out_specs=(VMEM, VMEM, VMEM),
        scratch_shapes=[
            pltpu.VMEM((units // part, part), jnp.int32),
            pltpu.VMEM(w_in.shape, BF16),
            pltpu.VMEM(w_out.shape, BF16),
            pltpu.SemaphoreType.DMA((3,)),
        ],
        compiler_params=params(),
        name="sort_units",
    )(core.reshape(1), *map(in_hbm, (unit_order.reshape(-1, part), w_in, w_out)))
    got = to_other_core(other)
    both = jnp.where(core == 0, jnp.concatenate([own, got], axis=3), jnp.concatenate([got, own], axis=3))
    mine = exchange(both)
    weights = lax.all_gather(mine.reshape(2 * UNITS, width), "z", axis=0, tiled=True)
    weights = weights.reshape(Z, MP, 2, HALF, width)

    send = pl.pallas_call(
        tokens_kernel,
        out_shape=struct(MP, 2, count, part),
        in_specs=[VMEM, VMEM],
        out_specs=VMEM,
        compiler_params=params(),
        name="combine_cotangents",
    )(features, cotangents)
    tokens = exchange(send)
    tokens = tokens.transpose(1, 2, 0, 3).reshape(2, count, full)
    peer_tokens = to_other_core(tokens)

    grads, out_other, hidden, grad_pre = pl.pallas_call(
        grads_kernel,
        out_shape=(
            struct(Z, MP, 2, HALF, width),
            struct(MP, 2, count, part),
            pltpu.VMEM((count, UNITS), BF16),
            pltpu.VMEM((count, UNITS), BF16),
        ),
        in_specs=[ANY] * 3,
        out_specs=(ANY,) * 4,
        scratch_shapes=[
            pltpu.VMEM((2 * count, full), BF16),
            pltpu.VMEM((2 * count, full), BF16),
            pltpu.VMEM((MP, HALF, full), BF16),
            pltpu.VMEM((MP, HALF, full), BF16),
            pltpu.VMEM((Z, MP, 2, HALF, width), BF16),
            pltpu.VMEM((MP, 2, count, part), BF16),
            pltpu.VMEM((2 * count, UNITS), BF16),
            pltpu.VMEM((2 * count, UNITS), BF16),
            pltpu.SemaphoreType.DMA((4,)),
            pltpu.SemaphoreType.DMA((2 * Z,)),
            pltpu.SemaphoreType.DMA((Z,)),
            pltpu.SemaphoreType.DMA((Z,)),
            pltpu.SemaphoreType.DMA((2,)),
        ],
        compiler_params=params(58),
        cost_estimate=pl.CostEstimate(
            flops=10 * UNITS * 2 * count * full, bytes_accessed=20 << 20, transcendentals=UNITS * 2 * count
        ),
        name="hidden_and_weight_grads",
    )(tokens, peer_tokens, weights)
    summed = lax.psum_scatter(grads.reshape(Z * 2 * UNITS, width), "z", scatter_dimension=0, tiled=True)
    summed = summed.reshape(MP, 2, HALF, width)

    out_own = pl.pallas_call(
        own_kernel,
        out_shape=struct(MP, 2, count, part),
        in_specs=[ANY] * 3,
        out_specs=ANY,
        scratch_shapes=[
            pltpu.VMEM((count, UNITS), BF16),
            pltpu.VMEM((count, UNITS), BF16),
            pltpu.VMEM((Z, MP, 2, HALF, width), BF16),
            pltpu.VMEM((MP, 2, count, part), BF16),
            pltpu.SemaphoreType.DMA((2,)),
            pltpu.SemaphoreType.DMA((Z,)),
            pltpu.SemaphoreType.DMA((Z,)),
        ],
        compiler_params=params(50),
        cost_estimate=pl.CostEstimate(flops=4 * UNITS * count * full, bytes_accessed=8 << 20, transcendentals=0),
        name="own_outputs_and_feature_grads",
    )(in_vmem(hidden), in_vmem(grad_pre), weights)
    out_peer = to_other_core(out_other)
    out_sum = (out_own.astype(F32) + out_peer.astype(F32)).astype(BF16)
    out_got = exchange(out_sum)
    rows = 128
    outputs, grad_features = pl.pallas_call(
        sums_kernel,
        grid=(count // rows,),
        out_shape=(struct(4, count, part), struct(count, part)),
        in_specs=[pl.BlockSpec((MP, 2, rows, part), lambda t: (0, 0, t, 0))],
        out_specs=(
            pl.BlockSpec((4, rows, part), lambda t: (0, t, 0)),
            pl.BlockSpec((rows, part), lambda t: (t, 0)),
        ),
        compiler_params=params(),
        name="sum_outputs",
    )(out_got)

    back = exchange(gate(summed, out_got))
    left, right = back[..., :part], back[..., part:]
    keep = jnp.where(core == 0, left, right)
    give = jnp.where(core == 0, right, left)
    grad_in, grad_out = pl.pallas_call(
        unsort_kernel,
        out_shape=(struct(part, units), struct(units, part)),
        in_specs=[VMEM, VMEM, VMEM],
        out_specs=(VMEM, VMEM),
        compiler_params=params(),
        name="unsort_grads",
    )(places, keep, to_other_core(give))
    return outputs, grad_features, grad_in, grad_out


def solution(mesh):
    whole = Mesh(mesh.devices.reshape(Z, 2, 4, 4), ("z", "core", "y", "x"))
    dp, mp = ("z", "core"), ("y", "x")
    return jax.shard_map(
        per_device,
        mesh=whole,
        in_specs=(P(dp, mp), P(dp, mp), P(mp, dp), P(mp), P(None, dp, mp)),
        out_specs=(P(None, dp, mp), P(dp, mp), P(dp, mp), P(mp, dp)),
        check_vma=False,
    )
```

```python
import functools

import jax
import jax.numpy as jnp
from jax import lax
from jax.experimental import pallas as pl
from jax.experimental.pallas import tpu as pltpu
from jax.sharding import Mesh, PartitionSpec as P

FF = 16384
MP = 16
Z = 8
SHARE = 64
HALF = SHARE // 2
UNITS = MP * HALF
LAST_OF_BAND = (1, 3, 7, 15)

tanh_scale = 0.7978845608
cubic_term = 0.044715

F32 = jnp.float32
BF16 = jnp.bfloat16
MXN = (((1,), (1,)), ((), ()))
TN = (((0,), (0,)), ((), ()))


def params(mib=24):
    return pltpu.CompilerParams(vmem_limit_bytes=mib << 20)


def one_hot(places):
    rows, lanes = places.shape
    number = lax.broadcasted_iota(jnp.int32, (rows * lanes, lanes), 0)
    return jnp.concatenate([(number == places[r : r + 1]).astype(BF16) for r in range(rows)], axis=1)


def sort_kernel(
    core_ref, units_hbm, w_in_hbm, w_out_hbm, own_ref, other_ref, places_ref,
    units_ref, w_in_ref, w_out_ref, load_sem,
):
    first, *loads = [
        pltpu.make_async_copy(units_hbm, units_ref, load_sem.at[0]),
        pltpu.make_async_copy(w_in_hbm, w_in_ref, load_sem.at[1]),
        pltpu.make_async_copy(w_out_hbm, w_out_ref, load_sem.at[2]),
    ]
    for load in (first, *loads):
        load.start()
    first.wait()
    units = units_ref[...]
    band = (
        (units >= FF // 8).astype(jnp.int32)
        + (units >= FF // 4).astype(jnp.int32)
        + (units >= FF // 2).astype(jnp.int32)
    )
    count, lanes = band.shape
    members = [band == b for b in range(4)]
    stacked = jnp.concatenate([member.astype(F32) for member in members], axis=0)
    before = (
        lax.broadcasted_iota(jnp.int32, (lanes, lanes), 0) < lax.broadcasted_iota(jnp.int32, (lanes, lanes), 1)
    ).astype(BF16)
    within_row = jnp.dot(stacked.astype(BF16), before, preferred_element_type=F32)
    totals = jnp.sum(stacked, axis=1, keepdims=True)
    size = count * lanes
    ranks = [jnp.zeros((1, lanes), F32)] * count
    for b, base in enumerate((0, size // 8, size // 4, size // 2)):
        so_far = jnp.full((1, 1), base, F32)
        for r in range(count):
            row = slice(b * count + r, b * count + r + 1)
            ranks[r] = ranks[r] + stacked[row] * (within_row[row] + so_far)
            so_far = so_far + totals[row]
    rank = jnp.concatenate(ranks, axis=0).astype(jnp.int32)
    dest = rank // SHARE
    within = rank % SHARE
    half = within // HALF
    places = jnp.where(half == core_ref[0], 0, UNITS) + dest * HALF + within % HALF
    places_ref[...] = places
    picks = one_hot(places)
    for load in loads:
        load.wait()
    rows_in = lax.dot_general(picks, w_in_ref[...], MXN, preferred_element_type=F32).astype(BF16)
    rows_out = jnp.dot(picks, w_out_ref[...], preferred_element_type=F32).astype(BF16)
    for k in range(MP):
        lo = k * HALF
        own_ref[k, 0] = rows_in[lo : lo + HALF]
        own_ref[k, 1] = rows_out[lo : lo + HALF]
        other_ref[k, 0] = rows_in[UNITS + lo : UNITS + lo + HALF]
        other_ref[k, 1] = rows_out[UNITS + lo : UNITS + lo + HALF]


def unsort_kernel(places_ref, own_ref, other_ref, grad_in_ref, grad_out_ref):
    picks = one_hot(places_ref[...])

    def rows(i):
        return jnp.concatenate([own_ref[k, i] for k in range(MP)] + [other_ref[k, i] for k in range(MP)], axis=0)

    grad_in_ref[...] = lax.dot_general(rows(0), picks, TN, preferred_element_type=F32).astype(BF16)
    grad_out_ref[...] = lax.dot_general(rows(1), picks, TN, preferred_element_type=F32).T.astype(BF16)


def tokens_kernel(x_ref, cot_ref, send_ref):
    x = x_ref[...]
    total = cot_ref[3].astype(F32)
    combined = [None] * 4
    combined[3] = cot_ref[3]
    for b in (2, 1, 0):
        total = total + cot_ref[b].astype(F32)
        combined[b] = total.astype(BF16)
    first = 0
    for b, last in enumerate(LAST_OF_BAND):
        for k in range(first, last + 1):
            send_ref[k, 0] = x
            send_ref[k, 1] = combined[b]
        first = last + 1


def project(left_hidden, left_grad, weights_of, result_ref, target_ref, store_sem):
    part = result_ref.shape[-1]
    stores = []
    for z in range(Z):
        w_in, w_out = weights_of(z)
        for i, (left, right) in enumerate(((left_hidden, w_out), (left_grad, w_in))):
            whole = jnp.dot(left, right, preferred_element_type=F32).astype(BF16)
            for half in range(2):
                result_ref[2 * z + half, i] = whole[:, half * part : (half + 1) * part]
        blocks = pl.ds(2 * z, 2)
        store = pltpu.make_async_copy(result_ref.at[blocks], target_ref.at[blocks], store_sem.at[z])
        store.start()
        stores.append(store)
    return stores


def grads_kernel(
    own_ref, peer_ref, weights_ref, grads_ref, other_ref, hidden_ref, grad_pre_ref,
    x_ref, comb_ref, in_ref, out_ref, part_ref, theirs_ref, hid_ref, gpre_ref,
    token_sem, weight_sem, grad_sem, store_sem, keep_sem,
):
    count = own_ref.shape[1]
    width = weights_ref.shape[-1]
    full = in_ref.shape[-1]
    loads = ([], [])
    for i, (tokens, weights) in enumerate(((x_ref, in_ref), (comb_ref, out_ref))):
        for half, ref in enumerate((own_ref, peer_ref)):
            loads[i].append(
                pltpu.make_async_copy(
                    ref.at[i], tokens.at[pl.ds(half * count, count)], token_sem.at[2 * half + i]
                )
            )
        for z in range(Z):
            loads[i].append(
                pltpu.make_async_copy(
                    weights_ref.at[z, :, i], weights.at[:, :, pl.ds(z * width, width)], weight_sem.at[2 * z + i]
                )
            )
    for load in loads[0] + loads[1]:
        load.start()
    products = []
    for i, (tokens, weights) in enumerate(((x_ref, in_ref), (comb_ref, out_ref))):
        for load in loads[i]:
            load.wait()
        weight = weights[...].reshape(UNITS, full)
        products.append(lax.dot_general(tokens[...], weight, MXN, preferred_element_type=F32))
    pre, back = products
    square = pre * pre
    tangent = jnp.tanh(tanh_scale * (pre + cubic_term * square * pre))
    hid_ref[...] = (0.5 * pre * (1.0 + tangent)).astype(BF16)
    slope = 0.5 * (1.0 + tangent) + 0.5 * pre * (1.0 - tangent * tangent) * tanh_scale * (
        1.0 + 3.0 * cubic_term * square
    )
    gpre_ref[...] = (back * slope).astype(BF16)
    copies = [
        pltpu.make_async_copy(hid_ref.at[pl.ds(0, count)], hidden_ref, keep_sem.at[0]),
        pltpu.make_async_copy(gpre_ref.at[pl.ds(0, count)], grad_pre_ref, keep_sem.at[1]),
    ]
    for copy in copies:
        copy.start()

    def weights_of(z):
        lanes = slice(z * width, (z + 1) * width)
        return [ref[:, :, lanes].reshape(UNITS, width) for ref in (in_ref, out_ref)]

    copies += project(hid_ref[count:], gpre_ref[count:], weights_of, theirs_ref, other_ref, store_sem)
    turned = [left[...].T for left in (gpre_ref, hid_ref)]
    for z in range(Z):
        lanes = slice(z * width, (z + 1) * width)
        for i, tokens in enumerate((x_ref, comb_ref)):
            grad = jnp.dot(turned[i], tokens[:, lanes], preferred_element_type=F32)
            part_ref[z, :, i] = grad.astype(BF16).reshape(MP, HALF, width)
        copy = pltpu.make_async_copy(part_ref.at[z], grads_ref.at[z], grad_sem.at[z])
        copy.start()
        copies.append(copy)
    for copy in copies:
        copy.wait()


def own_kernel(
    hidden_ref, grad_pre_ref, weights_ref, own_ref,
    hid_ref, gpre_ref, held_ref, mine_ref, load_sem, weight_sem, store_sem,
):
    width = weights_ref.shape[-1]
    loads = [
        pltpu.make_async_copy(hidden_ref, hid_ref, load_sem.at[0]),
        pltpu.make_async_copy(grad_pre_ref, gpre_ref, load_sem.at[1]),
    ]
    pieces = [pltpu.make_async_copy(weights_ref.at[z], held_ref.at[z], weight_sem.at[z]) for z in range(Z)]
    for load in loads + pieces:
        load.start()
    for load in loads:
        load.wait()

    def weights_of(z):
        pieces[z].wait()
        return [held_ref[z, :, i].reshape(UNITS, width) for i in range(2)]

    for store in project(hid_ref[...], gpre_ref[...], weights_of, mine_ref, own_ref, store_sem):
        store.wait()


def sums_kernel(got_ref, outputs_ref, dx_ref):
    total = jnp.zeros(dx_ref.shape, F32)
    for k in range(MP):
        total = total + got_ref[k, 0].astype(F32)
        if k in LAST_OF_BAND:
            outputs_ref[LAST_OF_BAND.index(k)] = total.astype(BF16)
    total = jnp.zeros(dx_ref.shape, F32)
    for k in range(MP):
        total = total + got_ref[k, 1].astype(F32)
    dx_ref[...] = total.astype(BF16)


ANY = pl.BlockSpec(memory_space=pl.ANY)
VMEM = pl.BlockSpec(memory_space=pltpu.VMEM)
SMEM = pl.BlockSpec(memory_space=pltpu.SMEM)


def struct(*shape, dtype=BF16):
    return jax.ShapeDtypeStruct(shape, dtype)


def in_hbm(value):
    return pltpu.with_memory_space_constraint(value, pltpu.HBM)


def in_vmem(value):
    return pltpu.with_memory_space_constraint(value, pltpu.VMEM)


def to_other_core(value):
    return lax.ppermute(value, "core", [(0, 1), (1, 0)])


def exchange(value):
    return lax.all_to_all(value, ("y", "x"), 0, 0, tiled=True)


def gate_kernel(*refs):
    del refs


def gate(value, earlier):
    return pl.pallas_call(
        gate_kernel,
        out_shape=struct(*value.shape),
        in_specs=[ANY, ANY],
        out_specs=ANY,
        input_output_aliases={0: 0},
        name="gate",
    )(in_hbm(value), earlier)


def per_device(features, w_in, w_out, unit_order, cotangents):
    core = lax.axis_index("core")
    count, part = features.shape
    units = unit_order.shape[0]
    width = 2 * part
    full = MP * part
    own, other, places = pl.pallas_call(
        sort_kernel,
        out_shape=(
            struct(MP, 2, HALF, part),
            struct(MP, 2, HALF, part),
            struct(units // part, part, dtype=jnp.int32),
        ),
        in_specs=[SMEM, ANY, ANY, ANY],
        out_specs=(VMEM, VMEM, VMEM),
        scratch_shapes=[
            pltpu.VMEM((units // part, part), jnp.int32),
            pltpu.VMEM(w_in.shape, BF16),
            pltpu.VMEM(w_out.shape, BF16),
            pltpu.SemaphoreType.DMA((3,)),
        ],
        compiler_params=params(),
        name="sort_units",
    )(core.reshape(1), *map(in_hbm, (unit_order.reshape(-1, part), w_in, w_out)))
    got = to_other_core(other)
    both = jnp.where(core == 0, jnp.concatenate([own, got], axis=3), jnp.concatenate([got, own], axis=3))
    mine = exchange(both)
    weights = lax.all_gather(mine.reshape(2 * UNITS, width), "z", axis=0, tiled=True)
    weights = weights.reshape(Z, MP, 2, HALF, width)

    send = pl.pallas_call(
        tokens_kernel,
        out_shape=struct(MP, 2, count, part),
        in_specs=[VMEM, VMEM],
        out_specs=VMEM,
        compiler_params=params(),
        name="combine_cotangents",
    )(features, cotangents)
    tokens = exchange(send)
    tokens = tokens.transpose(1, 2, 0, 3).reshape(2, count, full)
    peer_tokens = to_other_core(tokens)

    grads, out_other, hidden, grad_pre = pl.pallas_call(
        grads_kernel,
        out_shape=(
            struct(Z, MP, 2, HALF, width),
            struct(MP, 2, count, part),
            pltpu.VMEM((count, UNITS), BF16),
            pltpu.VMEM((count, UNITS), BF16),
        ),
        in_specs=[ANY] * 3,
        out_specs=(ANY,) * 4,
        scratch_shapes=[
            pltpu.VMEM((2 * count, full), BF16),
            pltpu.VMEM((2 * count, full), BF16),
            pltpu.VMEM((MP, HALF, full), BF16),
            pltpu.VMEM((MP, HALF, full), BF16),
            pltpu.VMEM((Z, MP, 2, HALF, width), BF16),
            pltpu.VMEM((MP, 2, count, part), BF16),
            pltpu.VMEM((2 * count, UNITS), BF16),
            pltpu.VMEM((2 * count, UNITS), BF16),
            pltpu.SemaphoreType.DMA((4,)),
            pltpu.SemaphoreType.DMA((2 * Z,)),
            pltpu.SemaphoreType.DMA((Z,)),
            pltpu.SemaphoreType.DMA((Z,)),
            pltpu.SemaphoreType.DMA((2,)),
        ],
        compiler_params=params(58),
        cost_estimate=pl.CostEstimate(
            flops=10 * UNITS * 2 * count * full, bytes_accessed=20 << 20, transcendentals=UNITS * 2 * count
        ),
        name="hidden_and_weight_grads",
    )(tokens, peer_tokens, weights)
    summed = lax.psum_scatter(grads.reshape(Z * 2 * UNITS, width), "z", scatter_dimension=0, tiled=True)
    summed = summed.reshape(MP, 2, HALF, width)

    out_own = pl.pallas_call(
        own_kernel,
        out_shape=struct(MP, 2, count, part),
        in_specs=[ANY] * 3,
        out_specs=ANY,
        scratch_shapes=[
            pltpu.VMEM((count, UNITS), BF16),
            pltpu.VMEM((count, UNITS), BF16),
            pltpu.VMEM((Z, MP, 2, HALF, width), BF16),
            pltpu.VMEM((MP, 2, count, part), BF16),
            pltpu.SemaphoreType.DMA((2,)),
            pltpu.SemaphoreType.DMA((Z,)),
            pltpu.SemaphoreType.DMA((Z,)),
        ],
        compiler_params=params(50),
        cost_estimate=pl.CostEstimate(flops=4 * UNITS * count * full, bytes_accessed=8 << 20, transcendentals=0),
        name="own_outputs_and_feature_grads",
    )(in_vmem(hidden), in_vmem(grad_pre), weights)
    out_peer = to_other_core(out_other)
    out_sum = (out_own.astype(F32) + out_peer.astype(F32)).astype(BF16)
    out_got = exchange(out_sum)
    outputs, grad_features = pl.pallas_call(
        sums_kernel,
        out_shape=(struct(4, count, part), struct(count, part)),
        in_specs=[VMEM],
        out_specs=(VMEM, VMEM),
        compiler_params=params(),
        name="sum_outputs",
    )(out_got)

    back = exchange(gate(summed, out_got))
    left, right = back[..., :part], back[..., part:]
    keep = jnp.where(core == 0, left, right)
    give = jnp.where(core == 0, right, left)
    grad_in, grad_out = pl.pallas_call(
        unsort_kernel,
        out_shape=(struct(part, units), struct(units, part)),
        in_specs=[VMEM, VMEM, VMEM],
        out_specs=(VMEM, VMEM),
        compiler_params=params(),
        name="unsort_grads",
    )(places, keep, to_other_core(give))
    return outputs, grad_features, grad_in, grad_out


def solution(mesh):
    whole = Mesh(mesh.devices.reshape(Z, 2, 4, 4), ("z", "core", "y", "x"))
    dp, mp = ("z", "core"), ("y", "x")
    return jax.shard_map(
        per_device,
        mesh=whole,
        in_specs=(P(dp, mp), P(dp, mp), P(mp, dp), P(mp), P(None, dp, mp)),
        out_specs=(P(None, dp, mp), P(dp, mp), P(dp, mp), P(mp, dp)),
        check_vma=False,
    )
```
